32 devices in a mesh: section: 2 (over x), dp: 16 (over z, y, core).
Axes of the slice: x: 2, y: 2, z: 4, core: 2. Of those that a mesh axis runs over, the one named last changes fastest.
Arguments:
- features: bfloat16 [2, 16, 784, 256], P('section', 'dp'), may hold values from -6 to 6
- crop_side: int32 [2], replicated, may hold values from 20 to 28, as said below
- tag_ids: int32 [2, 16, 512], P(None, 'dp'), may hold values from 0 to 31
- tag_count: int32 [2, 16], P(None, 'dp'), may hold values from 256 to 512, as said below
- cell_pick: int32 [2, 16, 256], P(None, 'dp'), may hold values from 0 to 32767
- box_units: int32 [2, 16, 4, 256], P(None, 'dp'), may hold values from 0 to 1023
- conv_first: bfloat16 [2304, 256], replicated, may hold values from -0.125 to 0.125
- conv_first_bias: float32 [256], replicated, may hold values from -3 to 3
- conv_second: bfloat16 [2304, 256], replicated, may hold values from -0.125 to 0.125
- conv_second_bias: float32 [256], replicated, may hold values from -3 to 3
- projection: bfloat16 [256, 512], replicated, may hold values from -0.375 to 0.375
- projection_bias: float32 [512], replicated, may hold values from -3 to 3
- encoder_attention: bfloat16 [512, 1536], replicated, may hold values from -0.25 to 0.25
- encoder_output: bfloat16 [512, 512], replicated, may hold values from -1 to 1
- attention_gain: float32 [512], replicated, may hold values from 0.5 to 1.5
- attention_shift: float32 [512], replicated, may hold values from -3 to 3
- encoder_up: bfloat16 [512, 1024], replicated, may hold values from -0.25 to 0.25
- encoder_up_bias: float32 [1024], replicated, may hold values from -3 to 3
- encoder_down: bfloat16 [1024, 512], replicated, may hold values from -0.1875 to 0.1875
- encoder_down_bias: float32 [512], replicated, may hold values from -3 to 3
- feedforward_gain: float32 [512], replicated, may hold values from 0.5 to 1.5
- feedforward_shift: float32 [512], replicated, may hold values from -3 to 3
- tag_table: bfloat16 [32, 512], replicated, may hold values from -6 to 6
- decoder_attention: bfloat16 [512, 1536], replicated, may hold values from -0.25 to 0.25
- decoder_output: bfloat16 [512, 512], replicated, may hold values from -1 to 1
- decoder_query: bfloat16 [512, 512], replicated, may hold values from -0.25 to 0.25
- decoder_memory: bfloat16 [512, 1024], replicated, may hold values from -0.25 to 0.25
- decoder_cross: bfloat16 [512, 512], replicated, may hold values from -1 to 1
- decoder_up: bfloat16 [512, 1024], replicated, may hold values from -0.25 to 0.25
- decoder_up_bias: float32 [1024], replicated, may hold values from -3 to 3
- decoder_down: bfloat16 [1024, 512], replicated, may hold values from -0.1875 to 0.1875
- decoder_down_bias: float32 [512], replicated, may hold values from -3 to 3
- decoder_gain: float32 [3, 512], replicated, may hold values from 0.5 to 1.5
- decoder_shift: float32 [3, 512], replicated, may hold values from -3 to 3
- box_query: bfloat16 [512, 512], replicated, may hold values from -0.25 to 0.25
- box_memory: bfloat16 [512, 1024], replicated, may hold values from -0.25 to 0.25
- box_output: bfloat16 [512, 512], replicated, may hold values from -1 to 1
- box_hidden: bfloat16 [512, 512], replicated, may hold values from -0.25 to 0.25
- box_hidden_bias: float32 [512], replicated, may hold values from -3 to 3
- box_coord: bfloat16 [512, 4], replicated, may hold values from -0.25 to 0.25
Outputs:
- boxes: float32 [2, 16, 4, 256], P('section', 'dp')
- input_grad: bfloat16 [2, 16, 784, 256], P('section', 'dp')
- grad_conv_first: float32 [2304, 256], replicated
- grad_conv_first_bias: float32 [256], replicated
- grad_conv_second: float32 [2304, 256], replicated
- grad_conv_second_bias: float32 [256], replicated
- grad_projection: float32 [256, 512], replicated
- grad_projection_bias: float32 [512], replicated
- grad_encoder_attention: float32 [512, 1536], replicated
- grad_encoder_output: float32 [512, 512], replicated
- grad_attention_gain: float32 [512], replicated
- grad_attention_shift: float32 [512], replicated
- grad_encoder_up: float32 [512, 1024], replicated
- grad_encoder_up_bias: float32 [1024], replicated
- grad_encoder_down: float32 [1024, 512], replicated
- grad_encoder_down_bias: float32 [512], replicated
- grad_feedforward_gain: float32 [512], replicated
- grad_feedforward_shift: float32 [512], replicated
- grad_tag_table: float32 [32, 512], replicated
- grad_decoder_attention: float32 [512, 1536], replicated
- grad_decoder_output: float32 [512, 512], replicated
- grad_decoder_query: float32 [512, 512], replicated
- grad_decoder_memory: float32 [512, 1024], replicated
- grad_decoder_cross: float32 [512, 512], replicated
- grad_decoder_up: float32 [512, 1024], replicated
- grad_decoder_up_bias: float32 [1024], replicated
- grad_decoder_down: float32 [1024, 512], replicated
- grad_decoder_down_bias: float32 [512], replicated
- grad_decoder_gain: float32 [3, 512], replicated
- grad_decoder_shift: float32 [3, 512], replicated
- grad_box_query: float32 [512, 512], replicated
- grad_box_memory: float32 [512, 1024], replicated
- grad_box_output: float32 [512, 512], replicated
- grad_box_hidden: float32 [512, 512], replicated
- grad_box_hidden_bias: float32 [512], replicated
- grad_box_coord: float32 [512, 4], replicated
The draws below stay inside these ranges and needn't reach their ends.
Inputs may be any that keep to these rules, and one draw needn't show every extreme that they name: `crop_side`: one micro-batch has crops of side 28; every other has a smaller side. `tag_count`: in every micro-batch some table has all 512 tags live.
All inputs are finite; a program needn't handle non-finite values.
Results may differ from the reference program's by a relative error of at most 0.025.
Values may be sent and summed in bfloat16 or wider, within the bound.
A program may use at most 384 MiB of HBM per device.

```python
import math
import jax
import jax.numpy as jnp
from jax import lax

D = 512
HEADS = 8
FF = 1024
C_IN = 256
VOCAB = 32
GRID = 28
SIDE = 20
TAG_LEN = 512
CELLS = 256
L = 784
MICRO = 2
IMAGES = 16


def draw_crop_side(key, part):
    key = jax.random.fold_in(key, 11)
    first_key, second_key = jax.random.split(key)
    smaller = jax.random.randint(first_key, (MICRO,), SIDE, GRID)
    forced = jax.random.randint(second_key, (), 0, MICRO)
    positions = jnp.arange(MICRO)
    return jnp.where(positions == forced, GRID, smaller).astype(jnp.int32)


def draw_tag_count(key, part):
    key = jax.random.fold_in(key, 23)
    first_key, second_key = jax.random.split(key)
    lengths = jax.random.randint(first_key, (MICRO, IMAGES), TAG_LEN // 2, TAG_LEN + 1)
    forced = jax.random.randint(second_key, (MICRO,), 0, IMAGES)
    filled = jnp.where(jnp.arange(IMAGES)[None, :] == forced[:, None], TAG_LEN, lengths)
    return filled.astype(jnp.int32)


def set_ends(values, key, low, largest):
    longest = values.shape.index(max(values.shape))
    spots = []
    for shift in (0, 1):
        where = [jax.random.randint(jax.random.fold_in(key, axis), (), 0, length) for axis, length in enumerate(values.shape)]
        where[longest] = (where[longest] + shift) % values.shape[longest]
        spots.append(tuple(where))
    return values.at[spots[0]].set(low).at[spots[1]].set(largest)


def steps_of(key, shape, shards, least, top_value):
    gain = 1.0
    for position, blocks in shards:
        steps = jax.random.uniform(jax.random.fold_in(jax.random.fold_in(key, 6), position), (blocks,), jnp.float32, least / len(shards), top_value / len(shards))
        gain = gain * jnp.repeat(jnp.exp(steps), shape[position] // blocks).reshape((-1,) + (1,) * (len(shape) - 1 - position))
    return gain


def noise(stream_key, extent, scale, most, cuts=(), kind=jnp.bfloat16):
    entries = scale * jax.random.normal(stream_key, extent, jnp.float32)
    if cuts:
        entries = entries * steps_of(stream_key, extent, cuts, -0.22, 0.18)
    return jnp.clip(entries, -most, most).astype(kind)


def setup_inputs(seed: int = 0) -> dict:
    keys = jax.random.split(jax.random.key(seed), 41)
    return {
        "features": noise(keys[0], (MICRO, IMAGES, L, C_IN), 1.0, 6.0, ((0, 2), (1, 16))),
        "crop_side": draw_crop_side(jax.random.fold_in(keys[40], 71), 0),
        "tag_ids": set_ends(jax.random.randint(keys[2], (MICRO, IMAGES, TAG_LEN), 0, VOCAB), jax.random.fold_in(keys[2], 1), 0, VOCAB - 1).astype(jnp.int32),
        "tag_count": draw_tag_count(jax.random.fold_in(keys[40], 71), 0),
        "cell_pick": set_ends(jax.random.randint(keys[4], (MICRO, IMAGES, CELLS), 0, 32768), jax.random.fold_in(keys[4], 1), 0, 32767).astype(jnp.int32),
        "box_units": set_ends(jax.random.randint(keys[5], (MICRO, IMAGES, 4, CELLS), 0, 1024), jax.random.fold_in(keys[5], 1), 0, 1023).astype(jnp.int32),
        "conv_first": noise(keys[6], (9 * C_IN, C_IN), (9 * C_IN) ** -0.5, 0.125),
        "conv_first_bias": noise(keys[7], (C_IN,), 0.3, 3.0, (), jnp.float32),
        "conv_second": noise(keys[8], (9 * C_IN, C_IN), (9 * C_IN) ** -0.5, 0.125),
        "conv_second_bias": noise(keys[9], (C_IN,), 0.3, 3.0, (), jnp.float32),
        "projection": noise(keys[10], (C_IN, D), C_IN ** -0.5, 0.375),
        "projection_bias": noise(keys[11], (D,), 0.3, 3.0, (), jnp.float32),
        "encoder_attention": noise(keys[12], (D, 3 * D), D ** -0.5, 0.25),
        "encoder_output": noise(keys[13], (D, D), (D // 16) ** -0.5, 1.0),
        "attention_gain": jnp.clip(1.0 + 0.1 * jax.random.normal(keys[14], (D,), jnp.float32), 0.5, 1.5),
        "attention_shift": noise(keys[15], (D,), 0.3, 3.0, (), jnp.float32),
        "encoder_up": noise(keys[16], (D, FF), D ** -0.5, 0.25),
        "encoder_up_bias": noise(keys[17], (FF,), 0.3, 3.0, (), jnp.float32),
        "encoder_down": noise(keys[18], (FF, D), FF ** -0.5, 0.1875),
        "encoder_down_bias": noise(keys[19], (D,), 0.3, 3.0, (), jnp.float32),
        "feedforward_gain": jnp.clip(1.0 + 0.1 * jax.random.normal(keys[20], (D,), jnp.float32), 0.5, 1.5),
        "feedforward_shift": noise(keys[21], (D,), 0.3, 3.0, (), jnp.float32),
        "tag_table": noise(keys[22], (VOCAB, D), 1.0, 6.0),
        "decoder_attention": noise(keys[23], (D, 3 * D), D ** -0.5, 0.25),
        "decoder_output": noise(keys[24], (D, D), (D // 16) ** -0.5, 1.0),
        "decoder_query": noise(keys[25], (D, D), D ** -0.5, 0.25),
        "decoder_memory": noise(keys[26], (D, 2 * D), D ** -0.5, 0.25),
        "decoder_cross": noise(keys[27], (D, D), (D // 16) ** -0.5, 1.0),
        "decoder_up": noise(keys[28], (D, FF), D ** -0.5, 0.25),
        "decoder_up_bias": noise(keys[29], (FF,), 0.3, 3.0, (), jnp.float32),
        "decoder_down": noise(keys[30], (FF, D), FF ** -0.5, 0.1875),
        "decoder_down_bias": noise(keys[31], (D,), 0.3, 3.0, (), jnp.float32),
        "decoder_gain": jnp.clip(1.0 + 0.1 * jax.random.normal(keys[32], (3, D), jnp.float32), 0.5, 1.5),
        "decoder_shift": noise(keys[33], (3, D), 0.3, 3.0, (), jnp.float32),
        "box_query": noise(keys[34], (D, D), D ** -0.5, 0.25),
        "box_memory": noise(keys[35], (D, 2 * D), D ** -0.5, 0.25),
        "box_output": noise(keys[36], (D, D), (D // 16) ** -0.5, 1.0),
        "box_hidden": noise(keys[37], (D, D), D ** -0.5, 0.25),
        "box_hidden_bias": noise(keys[38], (D,), 0.3, 3.0, (), jnp.float32),
        "box_coord": noise(keys[39], (D, 4), D ** -0.5, 0.25),
    }


@jax.custom_vjp
def low(v):
    return lax.optimization_barrier(v.astype(jnp.bfloat16)).astype(jnp.float32)

@jax.custom_vjp
def low_back(v):
    return v

def low_keep(v):
    return (low(v), None)

def low_pass(kept, grad):
    return (grad,)

def back_keep(v):
    return (v, None)

def back_low(kept, grad):
    return (low(grad),)
low.defvjp(low_keep, low_pass)
low_back.defvjp(back_keep, back_low)

def matmul(first_operand, second_operand):
    return jnp.dot(first_operand, second_operand, precision=lax.Precision.HIGHEST, preferred_element_type=jnp.float32)

def contract(pattern, first_operand, second_operand):
    return jnp.einsum(pattern, first_operand, second_operand, precision=lax.Precision.HIGHEST, preferred_element_type=jnp.float32)

def linear(values_in, weight):
    return low_back(matmul(low(values_in), weight))

def layer_norm(values_in, scaling, biasing):
    centre = values_in - lax.optimization_barrier(jnp.mean(values_in, axis=-1, keepdims=True))
    spread = lax.optimization_barrier(jnp.mean(centre * centre, axis=-1, keepdims=True))
    return centre * lax.rsqrt(spread + 1e-05) * scaling + biasing

def position_table(row_count, full_width):
    places = jnp.arange(row_count, dtype=jnp.float32)[:, None]
    factor = jnp.exp(jnp.arange(full_width // 2, dtype=jnp.float32) * (-2.0 * math.log(10000.0) / full_width))
    angles = places * factor[None, :]
    return jnp.concatenate([jnp.sin(angles), jnp.cos(angles)], axis=1)

def image_mask(crop_size):
    positions = jnp.arange(GRID * GRID, dtype=jnp.int32)
    return ((positions // GRID < crop_size) & (positions % GRID < crop_size)).astype(jnp.float32)

def conv_three(field, weight):
    channels = field.shape[1]
    padded = jnp.pad(field.reshape(GRID, GRID, channels), ((1, 1), (1, 1), (0, 0)))
    shifted = [padded[offset_y:offset_y + GRID, offset_x:offset_x + GRID] for offset_y in range(3) for offset_x in range(3)]
    return matmul(jnp.concatenate(shifted, axis=2).reshape(GRID * GRID, 9 * channels), weight)

def attend(queries, key_rows, value_rows, key_valid, causal, head_count):
    row_count, full_width = queries.shape
    key_count = key_rows.shape[0]
    head_size = full_width // head_count
    score_scale = head_size ** (-0.5)
    query_low = low(queries).reshape(row_count, head_count, head_size)
    key_low = low(key_rows).reshape(key_count, head_count, head_size)
    value_low = low(value_rows).reshape(key_count, head_count, head_size)
    blocks = 2 if row_count >= 1024 else 1
    block_rows = row_count // blocks
    starts = jnp.arange(blocks, dtype=jnp.int32) * block_rows
    key_index = jnp.arange(key_count, dtype=jnp.int32)

    def one_block(block_item):
        query_part, start = block_item
        scores = low_back(contract('qhd,khd->hqk', query_part, key_low) * score_scale)
        allowed = jnp.broadcast_to(key_valid[None, :], (block_rows, key_count))
        if causal:
            allowed = allowed & (key_index[None, :] <= start + jnp.arange(block_rows, dtype=jnp.int32)[:, None])
        scores = jnp.where(allowed[None], scores, -1e+30)
        scores = scores - lax.optimization_barrier(jnp.max(scores, axis=-1, keepdims=True))
        weights = jnp.exp(scores)
        probabilities = low(weights / lax.optimization_barrier(jnp.sum(weights, axis=-1, keepdims=True)))
        return contract('hqk,khd->qhd', probabilities, value_low)
    output = lax.map(jax.checkpoint(one_block), (query_low.reshape(blocks, block_rows, head_count, head_size), starts))
    return low_back(output.reshape(row_count, full_width))

def self_attention(sequence, weight_in, weight_out, key_valid, causal):
    model_width = weight_out.shape[0]
    packed = linear(sequence, weight_in)
    context = attend(packed[:, :model_width], packed[:, model_width:2 * model_width], packed[:, 2 * model_width:], key_valid, causal, HEADS)
    return linear(context, weight_out)

def section_front(feature_map, crop_size, front_weights):
    conv_first, conv_first_bias, conv_second, conv_second_bias, projection, projection_bias, encoder_attention, encoder_output, attention_gain, attention_shift = front_weights
    inside = image_mask(crop_size)
    tokens_in = feature_map * inside[:, None]
    hidden_first = jax.nn.gelu(low_back(conv_three(low(tokens_in), conv_first)) + conv_first_bias, approximate=False) * inside[:, None]
    hidden_second = jax.nn.gelu(low_back(conv_three(low(hidden_first), conv_second)) + conv_second_bias + tokens_in, approximate=False) * inside[:, None]
    encoded = linear(hidden_second, projection) + projection_bias + position_table(GRID * GRID, projection.shape[1])
    attended = self_attention(encoded, encoder_attention, encoder_output, inside > 0.5, False)
    return layer_norm(encoded + attended, attention_gain, attention_shift)

def section_back(memory_in, crop_size, tag_row, tag_total, pick_row, unit_rows, back_weights):
    encoder_up, encoder_up_bias, encoder_down, encoder_down_bias, feedforward_gain, feedforward_shift, tag_table, decoder_attention, decoder_output, decoder_query, decoder_memory, decoder_cross, decoder_up, decoder_up_bias, decoder_down, decoder_down_bias, decoder_gain, decoder_shift, box_query, box_memory, box_output, box_hidden, box_hidden_bias, box_coord = back_weights
    model_width = decoder_query.shape[0]
    inside = image_mask(crop_size) > 0.5
    widened = jax.nn.gelu(linear(memory_in, encoder_up) + encoder_up_bias, approximate=False)
    memory = low(layer_norm(memory_in + linear(widened, encoder_down) + encoder_down_bias, feedforward_gain, feedforward_shift))
    tag_length = tag_row.shape[0]
    one_hot = (tag_row[:, None] == jnp.arange(tag_table.shape[0], dtype=jnp.int32)[None, :]).astype(jnp.float32)
    embedded = low_back(matmul(one_hot, tag_table)) + position_table(tag_length, model_width)
    tag_valid = jnp.ones((tag_length,), dtype=bool)
    first_stream = layer_norm(embedded + self_attention(embedded, decoder_attention, decoder_output, tag_valid, True), decoder_gain[0], decoder_shift[0])
    memory_pairs = low_back(matmul(memory, decoder_memory))
    cross_context = attend(linear(first_stream, decoder_query), memory_pairs[:, :model_width], memory_pairs[:, model_width:], inside, False, HEADS)
    second_stream = layer_norm(first_stream + linear(cross_context, decoder_cross), decoder_gain[1], decoder_shift[1])
    widened_tags = jax.nn.gelu(linear(second_stream, decoder_up) + decoder_up_bias, approximate=False)
    third_stream = layer_norm(second_stream + linear(widened_tags, decoder_down) + decoder_down_bias, decoder_gain[2], decoder_shift[2])
    cell_place = pick_row * tag_total // 32768
    cell_rows = jnp.take(third_stream, cell_place, axis=0)
    box_pairs = low_back(matmul(memory, box_memory))
    box_context = attend(linear(cell_rows, box_query), box_pairs[:, :model_width], box_pairs[:, model_width:], inside, False, 1)
    enriched = cell_rows + linear(box_context, box_output)
    hidden_rows = jax.nn.gelu(linear(enriched, box_hidden) + box_hidden_bias, approximate=False)
    predicted = jax.nn.sigmoid(linear(hidden_rows, box_coord))
    target = jnp.transpose(unit_rows).astype(jnp.float32) / 1024.0
    missed = predicted - target
    loss_value = 0.25 * jnp.sum(jnp.sqrt(1.0 + 16.0 * missed * missed))
    return (loss_value, jnp.transpose(predicted))

def reference(features, crop_side, tag_ids, tag_count, cell_pick, box_units, conv_first, conv_first_bias, conv_second, conv_second_bias, projection, projection_bias, encoder_attention, encoder_output, attention_gain, attention_shift, encoder_up, encoder_up_bias, encoder_down, encoder_down_bias, feedforward_gain, feedforward_shift, tag_table, decoder_attention, decoder_output, decoder_query, decoder_memory, decoder_cross, decoder_up, decoder_up_bias, decoder_down, decoder_down_bias, decoder_gain, decoder_shift, box_query, box_memory, box_output, box_hidden, box_hidden_bias, box_coord):
    front_weights = tuple((member.astype(jnp.float32) for member in (conv_first, conv_first_bias, conv_second, conv_second_bias, projection, projection_bias, encoder_attention, encoder_output, attention_gain, attention_shift)))
    back_weights = tuple((member.astype(jnp.float32) for member in (encoder_up, encoder_up_bias, encoder_down, encoder_down_bias, feedforward_gain, feedforward_shift, tag_table, decoder_attention, decoder_output, decoder_query, decoder_memory, decoder_cross, decoder_up, decoder_up_bias, decoder_down, decoder_down_bias, decoder_gain, decoder_shift, box_query, box_memory, box_output, box_hidden, box_hidden_bias, box_coord)))
    image_total = MICRO * IMAGES
    sides = jnp.repeat(crop_side, IMAGES).astype(jnp.int32)
    tag_flat = tag_ids.reshape(image_total, TAG_LEN)
    count_flat = tag_count.reshape(image_total)
    pick_flat = cell_pick.reshape(image_total, CELLS)
    unit_flat = box_units.reshape(image_total, 4, CELLS)

    def forward(feature_all, front_now, back_now):

        def one_image(image_item):
            feature_map, crop_size, tag_row, tag_total, pick_row, unit_rows = image_item
            memory_in = low_back(low(section_front(feature_map, crop_size, front_now)))
            return section_back(memory_in, crop_size, tag_row, tag_total, pick_row, unit_rows, back_now)
        losses, predicted = lax.map(jax.checkpoint(one_image), (feature_all, sides, tag_flat, count_flat, pick_flat, unit_flat))
        return (jnp.sum(losses), predicted)
    feature_all = features.reshape(image_total, GRID * GRID, C_IN).astype(jnp.float32)
    loss_value, pullback, predicted = jax.vjp(forward, feature_all, front_weights, back_weights, has_aux=True)
    feature_grad, front_grad, back_grad = pullback(jnp.ones((), jnp.float32))
    grads = front_grad + back_grad
    return (predicted.reshape(MICRO, IMAGES, 4, CELLS), feature_grad.reshape(features.shape).astype(jnp.bfloat16), grads[0], grads[1], grads[2], grads[3], grads[4], grads[5], grads[6], grads[7], grads[8], grads[9], grads[10], grads[11], grads[12], grads[13], grads[14], grads[15], grads[16], grads[17], grads[18], grads[19], grads[20], grads[21], grads[22], grads[23], grads[24], grads[25], grads[26], grads[27], grads[28], grads[29], grads[30], grads[31], grads[32], grads[33])
```

```python
import functools
import math

import jax
import jax.numpy as jnp
import numpy as np
from jax import lax
from jax.experimental import pallas as pl
from jax.experimental.pallas import tpu as pltpu
from jax.sharding import PartitionSpec as P

HEADS = 8
GRID = 28
PITCH = 32
F32 = jnp.float32
BF16 = jnp.bfloat16
NEG = -1e30
SECTION = "section"
SPLIT = "dp"
PANEL = 256
VMEM_LIMIT = 60 * 1024 * 1024


def mm(a, b):
    return jnp.dot(a, b, preferred_element_type=F32)


def mm_nt(a, b):
    return lax.dot_general(a, b, (((1,), (1,)), ((), ())), preferred_element_type=F32)


def rows_loop(total, tile, body):
    def step(i, carry):
        body(pl.ds(pl.multiple_of(i * tile, tile), tile))
        return carry

    lax.fori_loop(0, total // tile, step, 0)


def rows_sum(total, tile, width, body, count=1):
    def step(i, carry):
        parts = body(pl.ds(pl.multiple_of(i * tile, tile), tile))
        return tuple(c + part for c, part in zip(carry, parts))

    zeros = tuple(jnp.zeros((8, width), F32) for _ in range(count))
    sums = lax.fori_loop(0, total // tile, step, zeros)
    return tuple(jnp.sum(s, axis=0, keepdims=True) for s in sums)


def eights(v):
    return jnp.sum(v.reshape(v.shape[0] // 8, 8, v.shape[1]), axis=0)


def gelu_pair(z):
    phi = 0.5 * (1.0 + lax.erf(z * 0.7071067811865476))
    bell = jnp.exp(z * z * -0.5) * 0.3989422804014327
    return z * phi, phi + z * bell


def inside_rows(start, rows, width, side):
    cell = lax.broadcasted_iota(jnp.int32, (rows, width), 0) + start
    return ((cell >> 5) < side) & ((cell & 31) < side)


def norm_forward(v, gain, shift):
    centre = v - jnp.mean(v, axis=-1, keepdims=True)
    spread = jnp.mean(centre * centre, axis=-1, keepdims=True)
    inv = lax.rsqrt(spread + 1e-05)
    normal = centre * inv
    return normal, inv, normal * gain + shift


def norm_backward(dy, normal, inv, gain):
    d = dy * gain
    return (
        d
        - jnp.mean(d, axis=-1, keepdims=True)
        - normal * jnp.mean(d * normal, axis=-1, keepdims=True)
    ) * inv


def no_tick(cost):
    pass


def put_panels(out, base, left, right, tick=no_tick, cost=0.0):
    rows = left.shape[0]
    panels = right.shape[1] // PANEL
    for c in range(panels):
        value = mm(left[...], right[:, c * PANEL : (c + 1) * PANEL])
        out[base + c * rows : base + (c + 1) * rows, :] = value.astype(BF16)
        tick(cost / panels)


def put_small(out, at, value):
    for c in range(value.shape[1] // PANEL):
        rows = value.shape[0]
        out[at + c * rows : at + (c + 1) * rows, :] = value[:, c * PANEL : (c + 1) * PANEL]
    return at + value.shape[0] * value.shape[1] // PANEL


def put_smalls(out, at, values):
    for value in values:
        at = put_small(out, at, value)
    return at


def lane_tiles(total):
    return [(s, min(256, total - s)) for s in range(0, total, 256)]


CHUNK = 128


def folded(v, how):
    return how(v.reshape(v.shape[0] // 8, 8, v.shape[1]), axis=0)


def scores_of(key_part, query_part, mask, causal, at, start, size):
    s = mm(key_part, query_part)
    if not causal:
        return s + mask[at : at + CHUNK, :size]
    if at + CHUNK <= start:
        return s
    key_at = lax.broadcasted_iota(jnp.int32, (CHUNK, size), 0) + at
    query_at = lax.broadcasted_iota(jnp.int32, (CHUNK, size), 1) + start
    return jnp.where(key_at <= query_at, s, NEG)


def attend_forward(keys, q_t, v_t, out_t, lse, mask, causal, s_s, w_s):
    key_count = keys.shape[0]

    def pair(hp, carry):
        lanes = pl.ds(pl.multiple_of(hp * 128, 128), 128)
        for j in range(2):
            rows = pl.ds(pl.multiple_of(hp * 128 + 64 * j, 64), 64)
            for start, size in lane_tiles(q_t.shape[1]):
                seen = min(start + size, key_count) if causal else key_count
                query_part = q_t[rows, start : start + size]
                top = None
                for at in range(0, seen, CHUNK):
                    key_part = keys[at : at + CHUNK, lanes][:, 64 * j : 64 * j + 64]
                    s = scores_of(key_part, query_part, mask, causal, at, start, size)
                    s_s[at : at + CHUNK, :size] = s
                    part = folded(s, jnp.max)
                    top = part if top is None else jnp.maximum(top, part)
                top = jnp.max(top, axis=0, keepdims=True)
                total = jnp.zeros((8, size), F32)
                for at in range(0, seen, CHUNK):
                    w = jnp.exp(s_s[at : at + CHUNK, :size] - top)
                    total = total + folded(w, jnp.sum)
                    w_s[at : at + CHUNK, :size] = w.astype(BF16)
                total = jnp.sum(total, axis=0, keepdims=True)
                out_t[rows, start : start + size] = mm(v_t[rows, :seen], w_s[:seen, :size]) / total
                lse[2 * hp + j, :, start : start + size] = top + jnp.log(total)
        return carry

    lax.fori_loop(0, HEADS // 2, pair, 0)


def attend_backward(keys, values, keys_t, q, q_t, do, do_t, out_t, lse, mask, causal, dk, dv, dq_t, p_s, ds_s, tick, cost):
    key_count = keys.shape[0]
    share = cost / (HEADS * (len(lane_tiles(q_t.shape[1])) + 1))

    for hp in range(HEADS // 2):
        lanes = slice(hp * 128, hp * 128 + 128)
        q_pair = q[:, lanes]
        do_pair = do[:, lanes]
        dks = []
        dvs = []
        for j in range(2):
            rows = slice(hp * 128 + 64 * j, hp * 128 + 64 * j + 64)
            part = slice(64 * j, 64 * j + 64)
            for start, size in lane_tiles(q_t.shape[1]):
                cols = slice(start, start + size)
                seen = min(start + size, key_count) if causal else key_count
                query_part = q_t[rows, cols]
                do_part = do_t[rows, cols]
                log_total = lse[2 * hp + j, :, cols]
                dsum = jnp.sum(do_part.astype(F32) * out_t[rows, cols], axis=0, keepdims=True)
                for at in range(0, seen, CHUNK):
                    chunk = slice(at, at + CHUNK)
                    s = scores_of(keys[chunk, lanes][:, part], query_part, mask, causal, at, start, size)
                    p = jnp.exp(s - log_total)
                    p_s[chunk, cols] = p.astype(BF16)
                    dp = mm(values[chunk, lanes][:, part], do_part)
                    ds_s[chunk, cols] = (p * (dp - dsum)).astype(BF16)
                if causal and seen < key_count:
                    p_s[seen:, cols] = jnp.zeros((key_count - seen, size), BF16)
                    ds_s[seen:, cols] = jnp.zeros((key_count - seen, size), BF16)
                dq_t[rows, cols] = (mm(keys_t[rows, :seen], ds_s[:seen, cols]) * 0.125).astype(BF16)
                tick(share)
            dks.append(mm(ds_s[...], q_pair[:, part]))
            dvs.append(mm(p_s[...], do_pair[:, part]))
            tick(share)
        dk[:, lanes] = jnp.concatenate(dks, axis=1).astype(BF16)
        dv[:, lanes] = jnp.concatenate(dvs, axis=1).astype(BF16)


def im2col(value, dst):
    n = value.shape[0]
    blank = jnp.zeros((PITCH, 3 * PANEL), BF16)
    dst[0:PITCH, :] = blank
    dst[n + PITCH : n + 2 * PITCH, :] = blank
    dst[PITCH : n + PITCH, 0:PANEL] = pltpu.roll(value, 1, 0).astype(BF16)
    dst[PITCH : n + PITCH, PANEL : 2 * PANEL] = value.astype(BF16)
    dst[PITCH : n + PITCH, 2 * PANEL :] = pltpu.roll(value, n - 1, 0).astype(BF16)


def conv_of(cols, w, n):
    return (
        mm(cols[0:n, :], w[0:768, :])
        + mm(cols[PITCH : n + PITCH, :], w[768:1536, :])
        + mm(cols[2 * PITCH : n + 2 * PITCH, :], w[1536:2304, :])
    )


def front_kernel(crop, feat, w1, b1, w2, b2, wp, bp, pos, e, y1, g1, y2, g2, wide, x, z, cols, need, done):
    n = x.shape[0]
    need(feat)
    wide[...] = feat[...].astype(F32)
    x[...] = jnp.zeros_like(x)
    for r in range(GRID):
        x[r * PITCH : r * PITCH + GRID, :] = wide[r * GRID : (r + 1) * GRID, :]
    s = own_side(crop)
    x[...] = jnp.where(inside_rows(0, n, PANEL, s), x[...], 0.0)
    im2col(x[...], cols)
    need(w1, b1)
    z[...] = conv_of(cols, w1, n)

    def first(rows):
        y, g = gelu_pair(z[rows, :] + b1[...])
        ins = inside_rows(rows.start, rows.size, PANEL, s)
        y = jnp.where(ins, y, 0.0)
        z[rows, :] = y
        y1[rows, :] = y.astype(BF16)
        g1[rows, :] = jnp.where(ins, g, 0.0).astype(BF16)

    rows_loop(n, 64, first)
    done(y1, g1)
    im2col(z[...], cols)
    need(w2, b2)
    z[...] = conv_of(cols, w2, n)

    def second(rows):
        y, g = gelu_pair(z[rows, :] + b2[...] + x[rows, :])
        ins = inside_rows(rows.start, rows.size, PANEL, s)
        y2[rows, :] = jnp.where(ins, y, 0.0).astype(BF16)
        g2[rows, :] = jnp.where(ins, g, 0.0).astype(BF16)

    rows_loop(n, 64, second)
    done(y2, g2)
    need(wp, bp, pos)
    for c in range(2):
        cut = slice(c * PANEL, (c + 1) * PANEL)
        e[:, cut] = mm(y2[...], wp[:, cut]) + bp[:, cut] + pos[:, cut]


def own_side(crop):
    return crop[lax.axis_index(SECTION)]


def fill_mask(mask, crop):
    n = mask.shape[0]
    side = own_side(crop)
    mask[...] = jnp.where(inside_rows(0, n, PANEL, side), 0.0, NEG)


def split_qkv(x, w, keys, q, q_t, v, v_t):
    for c in range(2):
        cut = slice(c * PANEL, (c + 1) * PANEL)
        part = (mm(x[...], w[:, c * PANEL : (c + 1) * PANEL]).astype(BF16) * 0.125).astype(BF16)
        q[:, cut] = part
        q_t[cut, :] = part.T
        keys[:, cut] = mm(x[...], w[:, 512 + c * PANEL : 512 + (c + 1) * PANEL]).astype(BF16)
        part = mm(x[...], w[:, 1024 + c * PANEL : 1024 + (c + 1) * PANEL]).astype(BF16)
        v[:, cut] = part
        v_t[cut, :] = part.T


def self_forward(xb, x, w, wo, gain, shift, q, keys, v, out_t, lse, normal, inv, h, mask, causal, q_t, v_t, z, s_s, w_s, need, done):
    need(w)
    split_qkv(xb, w, keys, q, q_t, v, v_t)
    done(xb, q, keys, v)
    attend_forward(keys, q_t, v_t, out_t, lse, mask, causal, s_s, w_s)
    done(out_t, lse)
    need(wo)
    z[...] = mm(out_t[...].astype(BF16).T, wo[...])

    def finish(rows):
        nn, ii, y = norm_forward(x[rows, :] + z[rows, :], gain[...], shift[...])
        normal[rows, :] = nn.astype(BF16)
        inv[rows, :] = ii
        h[rows, :] = y.astype(h.dtype)

    rows_loop(x.shape[0], 64, finish)


def encoder_attention_kernel(crop, e, w, wo, gain, shift, eb, q, keys, v, out_t, lse, normal, inv, h, mask, q_t, v_t, z, s_s, w_s, need, done):
    fill_mask(mask, crop)
    need(e, gain, shift)
    eb[...] = e[...].astype(BF16)
    self_forward(eb, e, w, wo, gain, shift, q, keys, v, out_t, lse, normal, inv, h, mask, False, q_t, v_t, z, s_s, w_s, need, done)


def encoder_feed_kernel(h, wu, bu, wd, bd, gain, shift, wm, wb, u, gu, normal, inv, memory, pairs, box_pairs, z, f, need, done):
    n = h.shape[0]
    need(h, wu, bu)
    for c in range(wu.shape[1] // 512):
        cut = slice(c * 512, (c + 1) * 512)
        z[...] = mm(h[...], wu[:, cut])

        def grow(rows):
            y, g = gelu_pair(z[rows, :] + bu[:, cut])
            u[rows, cut] = y.astype(BF16)
            gu[rows, cut] = g.astype(BF16)

        rows_loop(n, 64, grow)
    done(u, gu)
    need(wd, bd, gain, shift)
    f[...] = mm(u[...], wd[...])

    def finish(rows):
        nn, ii, y = norm_forward(h[rows, :].astype(F32) + f[rows, :] + bd[...], gain[...], shift[...])
        normal[rows, :] = nn.astype(BF16)
        inv[rows, :] = ii
        memory[rows, :] = y.astype(BF16)

    rows_loop(n, 64, finish)
    done(normal, inv, memory)
    need(wm)
    for c in range(2):
        cut = slice(c * 512, (c + 1) * 512)
        pairs[:, cut] = mm(memory[...], wm[:, cut]).astype(BF16)
    done(pairs)
    need(wb)
    for c in range(2):
        cut = slice(c * 512, (c + 1) * 512)
        box_pairs[:, cut] = mm(memory[...], wb[:, cut]).astype(BF16)


def hot_columns(row, rows):
    return (row == lax.broadcasted_iota(jnp.int32, (rows, row.shape[1]), 0)).astype(F32)


def tag_kernel(ids, table, pos, w, wo, gain, shift, t0b, q, keys, v, out_t, lse, normal, inv, t1, mask, q_t, v_t, z, s_s, w_s, t0, need, done):
    need(ids, table, pos, gain, shift)
    hot = hot_columns(ids[lax.axis_index(SECTION)], table.shape[0])
    t0[...] = mm(hot.T.astype(BF16), table[...]) + pos[...]
    t0b[...] = t0[...].astype(BF16)
    self_forward(t0b, t0, w, wo, gain.at[0:1, :], shift.at[0:1, :], q, keys, v, out_t, lse, normal, inv, t1, mask, True, q_t, v_t, z, s_s, w_s, need, done)


def cross_kernel(crop, t1, pairs, wq, wo, gain, shift, t1b, q, out_t, lse, normal, inv, t2, mask, q_t, v_t, z, s_s, w_s, need, done):
    fill_mask(mask, crop)
    need(t1, wq, gain, shift)
    t1b[...] = t1[...].astype(BF16)
    part = (mm(t1b[...], wq[...]).astype(BF16) * 0.125).astype(BF16)
    q[...] = part
    q_t[...] = part.T
    need(pairs)
    v_t[...] = pairs[:, 512:].T
    done(t1b, q)
    attend_forward(pairs, q_t, v_t, out_t, lse, mask, False, s_s, w_s)
    done(out_t, lse)
    need(wo)
    z[...] = mm(out_t[...].astype(BF16).T, wo[...])

    def finish(rows):
        nn, ii, y = norm_forward(t1[rows, :] + z[rows, :], gain[1:2, :], shift[1:2, :])
        normal[rows, :] = nn.astype(BF16)
        inv[rows, :] = ii
        t2[rows, :] = y

    rows_loop(t1.shape[0], 64, finish)


def scoped(body, refs, scratch, need, done):
    pl.run_scoped(
        lambda *work: body(*refs, *work, need=need, done=done), *[pltpu.VMEM(shape, dtype) for shape, dtype in scratch]
    )


def forward_kernel(counts, crop, *refs, need, done):
    groups, at = [], 0
    for count in counts:
        groups.append(refs[at : at + count])
        at += count
    front_in, att_in, feed_in, tag_in, cross_in, front_out, att_out, feed_out, tag_out, cross_out = groups
    e, t1 = refs[at:]
    (n, width), count = e.shape, t1.shape[0]
    big, tall = (n, width), (count, width)
    cells_in, channels = front_in[0].shape
    scoped(
        front_kernel, (crop, *front_in, e, *front_out),
        [((cells_in, channels), F32), ((n, channels), F32), ((n, channels), F32), ((n + 64, 3 * channels), BF16)], need, done,
    )
    scoped(
        encoder_attention_kernel, (crop, e, *att_in, *att_out),
        [((n, PANEL), F32), ((width, n), BF16), ((width, n), BF16), (big, F32), ((n, PANEL), F32), ((n, PANEL), BF16)], need, done,
    )
    h = att_out[-1]
    scoped(encoder_feed_kernel, (h, *feed_in, *feed_out), [(big, F32), (big, F32)], need, done)
    scoped(
        tag_kernel, (*tag_in, *tag_out, t1),
        [((8, 128), F32), ((width, count), BF16), ((width, count), BF16), (tall, F32), ((count, PANEL), F32), ((count, PANEL), BF16),
         (tall, F32)], need, done,
    )
    pairs, gain, shift = feed_out[-2], tag_in[-2], tag_in[-1]
    scoped(
        cross_kernel, (crop, t1, pairs, *cross_in, gain, shift, *cross_out),
        [((n, PANEL), F32), ((width, count), BF16), ((width, n), BF16), (tall, F32), ((n, PANEL), F32), ((n, PANEL), BF16)], need, done,
    )


def feed_backward(dy, dy_b, normal, inv, gain, u, gu, xb, wu, wd, g_up, g_down, small, dx_out, dz, dx, t_s, tick=no_tick):
    n, width = dy.shape

    def through(rows):
        d = dy[rows, :]
        nn = normal[rows, :].astype(F32)
        out = norm_backward(d, nn, inv[rows, :], gain[...])
        dx[rows, :] = out
        dy_b[rows, :] = out.astype(BF16)
        return eights(d * nn), eights(d), eights(out)

    at = put_smalls(small, 0, rows_sum(n, 64, width, through, 3))
    tick(1.5)
    for c in range(u.shape[1] // 512):
        cut = slice(c * 512, (c + 1) * 512)
        t_s[...] = u[:, cut].T
        for p in range(width // PANEL):
            value = mm(t_s[...], dy_b[:, p * PANEL : (p + 1) * PANEL])
            row = p * u.shape[1] + c * 512
            g_down[row : row + 512, :] = value.astype(BF16)
            tick(0.8)
        dx_out[...] = mm_nt(dy_b[...], wd[cut, :])
        tick(1.2)

        def narrow(rows):
            d = dx_out[rows, :] * gu[rows, cut].astype(F32)
            dz[rows, cut] = d.astype(BF16)
            return (eights(d),)

        at = put_small(small, at, rows_sum(n, 64, 512, narrow)[0])
        tick(0.6)
    t_s[...] = xb[...].T
    put_panels(g_up, 0, t_s, dz, tick, 3.0)
    dx_out[...] = dx[...] + mm_nt(dz[...], wu[...])
    tick(2.0)
    return at


def box_kernel(
    crop, totals, t2, wu, bu, wd, bd, gains, shifts, picks, units, pairs, memory, wq, wm, wo, wh, bh, wc_t,
    boxes, dt2, dmem, grads, ffn, small,
    t2b, u, gu, normal, inv, z, dz, dx, t_s, d3, db, hot, hot_t, cells, dcells, mask, p_s, dpairs, mem_t, box_done, tick,
):
    gain, shift = gains.at[2:3, :], shifts.at[2:3, :]
    section = lax.axis_index(SECTION)
    side = crop[section]
    count = t2.shape[0]
    t2b[...] = t2[...].astype(BF16)
    for c in range(wu.shape[1] // 512):
        cut = slice(c * 512, (c + 1) * 512)
        z[...] = mm(t2b[...], wu[:, cut])

        def grow(rows):
            y, g = gelu_pair(z[rows, :] + bu[:, cut])
            u[rows, cut] = y.astype(BF16)
            gu[rows, cut] = g.astype(BF16)

        rows_loop(count, 64, grow)
    z[...] = mm(u[...], wd[...])

    def finish(rows):
        nn, ii, y = norm_forward(t2[rows, :] + z[rows, :] + bd[...], gain[...], shift[...])
        normal[rows, :] = nn.astype(BF16)
        inv[rows, :] = ii
        d3[rows, :] = y

    rows_loop(count, 64, finish)
    place = (picks[section] * totals[pl.ds(section, 1), :]) >> 15
    hot_f = hot_columns(place, count)
    hot_t[...] = hot_f.astype(BF16)
    hot[...] = hot_f.T.astype(BF16)
    high = d3[...].astype(BF16)
    rest = (d3[...] - high.astype(F32)).astype(BF16)
    cells[...] = mm(hot[...], high) + mm(hot[...], rest)
    cells_b = cells[...].astype(BF16)
    queries = mm(cells_b, wq[...]).astype(BF16)
    scale = 512.0 ** (-0.5)
    cell = lax.broadcasted_iota(jnp.int32, mask.shape, 1)
    mask[...] = jnp.where(((cell >> 5) < side) & ((cell & 31) < side), 0.0, NEG)
    s = mm_nt(queries, pairs[:, :512]) * scale + mask[...]
    s = jnp.exp(s - jnp.max(s, axis=1, keepdims=True))
    p_s[...] = s / jnp.sum(s, axis=1, keepdims=True)
    p_b = p_s[...].astype(BF16)
    context = mm(p_b, pairs[:, 512:]).astype(BF16)
    enriched = cells[...] + mm(context, wo[...])
    enriched_b = enriched.astype(BF16)
    hidden, slope = gelu_pair(mm(enriched_b, wh[...]) + bh[...])
    hidden_b = hidden.astype(BF16)
    guess = 1.0 / (1.0 + jnp.exp(-mm_nt(wc_t[...], hidden_b)))
    boxes[...] = guess[0:4]
    guess = guess[0:4]
    missed = guess - units[section, 0].astype(F32) * (1.0 / 1024.0)
    dlogit = 4.0 * missed * lax.rsqrt(1.0 + 16.0 * missed * missed) * guess * (1.0 - guess)
    dlogit = jnp.concatenate([dlogit, jnp.zeros((12, dlogit.shape[1]), F32)], axis=0)
    dwc_t = mm(dlogit.astype(BF16), hidden_b)
    dhidden = mm(dlogit.T.astype(BF16), wc_t[...]) * slope
    dhidden_b = dhidden.astype(BF16)
    put_panels(grads, 0, enriched_b.T, dhidden_b)
    dcells[...] = mm_nt(dhidden_b, wh[...])
    dout_b = dcells[...].astype(BF16)
    put_panels(grads, 1024, context.T, dout_b)
    dcontext = mm_nt(dout_b, wo[...]).astype(BF16)
    dp = mm_nt(dcontext, pairs[:, 512:])
    p = p_s[...].astype(BF16).astype(F32)
    ds = (p * (dp - jnp.sum(dp * p, axis=1, keepdims=True))).astype(BF16)
    dqueries = (mm(ds, pairs[:, :512]) * scale).astype(BF16)
    dpairs[:, :512] = (mm(ds.T, queries) * scale).astype(BF16)
    dpairs[:, 512:] = mm(p_b.T, dcontext).astype(BF16)
    put_panels(grads, 2048, cells_b.T, dqueries)
    dcells[...] += mm_nt(dqueries, wq[...])
    mem_t[...] = memory[...].T
    put_panels(grads, 3072, mem_t, dpairs)
    box_done()
    dmem[...] = mm_nt(dpairs[...], wm[...])
    tick(1.0)
    high = dcells[...].astype(BF16)
    rest = (dcells[...] - high.astype(F32)).astype(BF16)
    d3[...] = mm(hot_t[...], high) + mm(hot_t[...], rest)
    up_rows = 512 * wu.shape[1] // PANEL
    small[...] = jnp.zeros_like(small)
    tick(0.6)
    at = feed_backward(
        d3, db, normal, inv, gain, u, gu, t2b, wu, wd,
        ffn.at[0:up_rows, :], ffn.at[up_rows : 2 * up_rows, :], small, dt2, dz, dx, t_s, lambda cost: tick(0.6 * cost),
    )
    put_smalls(small, at, (jnp.sum(dhidden, axis=0, keepdims=True), dwc_t[0:4]))


def norm_rows_backward(dy, normal, inv, gain, small, dx, dxb):
    def through(rows):
        d = dy[rows, :].astype(F32)
        nn = normal[rows, :].astype(F32)
        out = norm_backward(d, nn, inv[rows, :], gain[...])
        dx[rows, :] = out
        dxb[rows, :] = out.astype(BF16)
        return eights(d * nn), eights(d)

    small[...] = jnp.zeros_like(small)
    return put_smalls(small, 0, rows_sum(dy.shape[0], 64, dy.shape[1], through, 2))


def cross_backward_kernel(
    crop, dt2, dmem_in, normal, inv, gains, out_t, lse, q, pairs, t1b, memory, wq, wm, wo,
    dt1, dmem, grads, small,
    mask, dx, dxb, do, do_t, q_t, keys_t, dpairs, dq_t, p_s, ds_s, mem_t, tick,
):
    fill_mask(mask, crop)
    norm_rows_backward(dt2, normal, inv, gains.at[1:2, :], small, dx, dxb)
    tick(0.8)
    put_panels(grads, 0, out_t[...].astype(BF16), dxb, tick, 0.7)
    do[...] = mm_nt(dxb[...], wo[...]).astype(BF16)
    do_t[...] = do[...].T
    q_t[...] = q[...].T
    keys_t[...] = pairs[:, :512].T
    tick(1.2)
    attend_backward(
        pairs.at[:, 0:512], pairs.at[:, 512:1024], keys_t, q, q_t, do, do_t, out_t, lse, mask, False,
        dpairs.at[:, 0:512], dpairs.at[:, 512:1024], dq_t, p_s, ds_s, tick, 13.0,
    )
    dq = dq_t[...].T
    put_panels(grads, 1024, t1b[...].T, dq, tick, 0.8)
    dt1[...] = dx[...] + mm_nt(dq, wq[...])
    mem_t[...] = memory[...].T
    put_panels(grads, 2048, mem_t, dpairs, tick, 1.8)
    dmem[...] = dmem_in[...] + mm_nt(dpairs[...], wm[...])
    tick(1.5)


def self_backward(dy, normal, inv, gain, out_t, lse, q, keys, v, xb, w, wo, mask, causal, grads, small,
                  dx, dxb, do, do_t, q_t, keys_t, dqkv, dq_t, p_s, ds_s, tick, cost):
    at = norm_rows_backward(dy, normal, inv, gain, small, dx, dxb)
    tick(1.0)
    put_panels(grads, 0, out_t[...].astype(BF16), dxb, tick, 0.8)
    do[...] = mm_nt(dxb[...], wo[...]).astype(BF16)
    do_t[...] = do[...].T
    q_t[...] = q[...].T
    keys_t[...] = keys[...].T
    tick(1.2)
    attend_backward(
        keys, v, keys_t, q, q_t, do, do_t, out_t, lse, mask, causal,
        dqkv.at[:, 512:1024], dqkv.at[:, 1024:1536], dq_t, p_s, ds_s, tick, cost,
    )
    dqkv[:, 0:512] = dq_t[...].T
    put_panels(grads, 1024, xb[...].T, dqkv, tick, 2.4)
    dx[...] += mm_nt(dqkv[...], w[...])
    tick(1.5)
    return at


def tag_backward_kernel(
    dt1, normal, inv, gains, out_t, lse, q, keys, v, t0b, ids, w, wo,
    grads, small,
    mask, dx, dxb, do, do_t, q_t, keys_t, dqkv, dq_t, p_s, ds_s, tick,
):
    at = self_backward(
        dt1, normal, inv, gains.at[0:1, :], out_t, lse, q, keys, v, t0b, w, wo, mask, True, grads, small,
        dx, dxb, do, do_t, q_t, keys_t, dqkv, dq_t, p_s, ds_s, tick, 7.0,
    )
    vocab = (small.shape[0] - at) // 2
    hot = hot_columns(ids[lax.axis_index(SECTION)], 32).astype(BF16)
    put_small(small, at, mm(hot, dx[...].astype(BF16)))


def encoder_feed_backward_kernel(
    dmem, normal, inv, gain, u, gu, h, wu, wd,
    dh, grads, small,
    db, dz, dx, t_s, tick,
):
    up_rows = 512 * wu.shape[1] // PANEL
    small[...] = jnp.zeros_like(small)
    feed_backward(
        dmem, db, normal, inv, gain, u, gu, h, wu, wd,
        grads.at[0:up_rows, :], grads.at[up_rows : 2 * up_rows, :], small, dh, dz, dx, t_s, tick,
    )


def encoder_attention_backward_kernel(
    crop, dh, normal, inv, gain, out_t, lse, q, keys, v, eb, w, wo,
    de, grads, small,
    mask, dhb, dxb, do, do_t, q_t, keys_t, dqkv, dq_t, p_s, ds_s, tick,
):
    fill_mask(mask, crop)
    dhb[...] = dh[...].astype(BF16)
    self_backward(
        dhb, normal, inv, gain, out_t, lse, q, keys, v, eb, w, wo, mask, False, grads, small,
        de, dxb, do, do_t, q_t, keys_t, dqkv, dq_t, p_s, ds_s, tick, 22.0,
    )


def spread_rows(value, pad):
    n = value.shape[0]
    pad[0:PITCH, :] = jnp.zeros((PITCH, pad.shape[1]), BF16)
    pad[PITCH : n + PITCH, :] = value
    pad[n + PITCH :, :] = jnp.zeros((PITCH, pad.shape[1]), BF16)


def conv_weight_grad(value, dz_pad, grads, base, tick):
    n = value.shape[0]
    for dx in range(3):
        shifted = value if dx == 1 else pltpu.roll(value, (1 - dx) % n, 0)
        shifted_t = shifted.astype(BF16).T
        for dy in range(3):
            part = mm(shifted_t, dz_pad[(2 - dy) * PITCH : (2 - dy) * PITCH + n, :])
            at = base + (dy * 3 + dx) * PANEL
            grads[at : at + PANEL, :] = part.astype(BF16)
        tick(1.0)


def conv_input_grad(cols, w, n, tick):
    total = None
    for dy in range(3):
        for dx in range(3):
            tap = dy * 3 + dx
            rows = slice((2 - dy) * PITCH, (2 - dy) * PITCH + n)
            lanes = slice((2 - dx) * PANEL, (3 - dx) * PANEL)
            part = mm_nt(cols[rows, lanes], w[tap * PANEL : (tap + 1) * PANEL, :])
            total = part if total is None else total + part
    return total


def front_backward(
    crop, de, feat, y1, g1, y2, g2, w1, w2, wp, dfeat, grads_a, grads_b, small, done_a, done_b,
    deb, z, x, first_in, wide, cols, pad, tick,
):
    n = x.shape[0]
    s = own_side(crop)
    small[...] = jnp.zeros_like(small)

    def take(rows):
        d = de[rows, :]
        deb[rows, :] = d.astype(BF16)
        return (eights(d),)

    at = put_small(small, 0, rows_sum(n, 64, de.shape[1], take)[0])
    put_panels(grads_a, 0, y2[...].T, deb, tick, 0.6)
    z[...] = mm_nt(deb[...], wp[...])

    def second(rows):
        d = z[rows, :] * g2[rows, :].astype(F32)
        z[rows, :] = d
        return (eights(d),)

    at = put_small(small, at, rows_sum(n, 64, PANEL, second)[0])
    im2col(z[...], cols)
    spread_rows(z[...].astype(BF16), pad)
    x[...] = z[...]
    tick(1.0)
    conv_weight_grad(y1[...].astype(F32), pad, grads_a, 2 * wp.shape[0], tick)
    done_a()
    z[...] = conv_input_grad(cols, w2, n, tick)
    tick(2.5)

    def first(rows):
        d = z[rows, :] * g1[rows, :].astype(F32)
        z[rows, :] = d
        return (eights(d),)

    put_small(small, at, rows_sum(n, 64, PANEL, first)[0])
    spread_rows(z[...].astype(BF16), pad)
    wide[...] = feat[...].astype(F32)
    first_in[...] = jnp.zeros_like(first_in)
    for r in range(GRID):
        first_in[r * PITCH : r * PITCH + GRID, :] = wide[r * GRID : (r + 1) * GRID, :]
    first_in[...] = jnp.where(inside_rows(0, n, PANEL, s), first_in[...], 0.0)
    tick(1.0)
    conv_weight_grad(first_in[...], pad, grads_b, 0, tick)
    done_b()
    im2col(z[...], cols)
    tick(0.5)
    x[...] = jnp.where(inside_rows(0, n, PANEL, s), x[...] + conv_input_grad(cols, w1, n, tick), 0.0)
    tick(2.5)
    for r in range(GRID):
        wide[r * GRID : (r + 1) * GRID, :] = x[r * PITCH : r * PITCH + GRID, :]
    dfeat[...] = wide[...].astype(BF16)


class Mesh2:
    def __init__(self, sections, splits):
        self.sections, self.splits = sections, splits
        self.devices = sections * splits
        split_bits = [(SPLIT, 1 << i) for i in range(splits.bit_length() - 1)]
        section_bits = [(SECTION, 1 << i) for i in range(sections.bit_length() - 1)]
        self.core = split_bits[:1]
        self.rest = section_bits + split_bits[1:]
        self.unit = 16 * self.devices

    def orders(self):
        r = self.rest
        if len(r) < 3:
            return [(self.core + r, 1.0)]
        first, second, rest = r[0], r[1], r[2:]
        return [
            (self.core + [first, second] + rest, 0.38),
            (self.core + [rest[0], second, first] + rest[1:], 0.24),
            (self.core + [second, first] + rest, 0.38),
        ]

    def links(self, axis, stride):
        if (axis, stride) in self.core:
            return [(0, 1)]
        if axis == SPLIT and self.splits == 16 and stride > 2:
            return [(1, 1)] if stride == 4 else [(1, 1), (2, 2)]
        return [((axis, stride), 1)]

    def padded(self, rows):
        return -(-rows // self.unit) * self.unit

    def cut(self, rows):
        units = rows // self.unit
        streams, at, goal = [], 0, 0.0
        for order, part in self.orders():
            goal += part
            stop = int(round(goal * units))
            if stop > at:
                streams.append((order, at * self.unit, (stop - at) * self.unit))
            at = stop
        return streams


class Share:
    ICI = 45e3
    CORE = 300e3
    LATENCY = 1.8

    def __init__(self, mesh2, total_rows, own, local_sem, send_sem, recv_sem):
        self.mesh2 = mesh2
        self.own, self.local_sem, self.send_sem, self.recv_sem = own, local_sem, send_sem, recv_sem
        everyone = mesh2.core + mesh2.rest
        self.bits = len(everyone)
        place = {SECTION: lax.axis_index(SECTION), SPLIT: lax.axis_index(SPLIT)}
        self.bit_of, self.partner_of = {}, {}
        for axis, stride in everyone:
            bit = lax.rem(lax.div(place[axis], np.int32(stride)), np.int32(2))
            moved = dict(place)
            moved[axis] = moved[axis] + stride - 2 * stride * bit
            self.bit_of[(axis, stride)] = bit
            self.partner_of[(axis, stride)] = (moved[SECTION], moved[SPLIT])
        self.streams = []
        self.own_rows = 0
        self.clock = 0.0
        self.free = {}
        self.queue = []

    def bit(self, axis, stride):
        return self.bit_of[(axis, stride)]

    def partner(self, axis, stride):
        return self.partner_of[(axis, stride)]

    def enter(self):
        barrier = pltpu.get_barrier_semaphore()
        everyone = self.mesh2.core + self.mesh2.rest
        for axis, stride in everyone:
            pl.semaphore_signal(
                barrier, inc=1, device_id=self.partner(axis, stride), device_id_type=pl.DeviceIdType.MESH
            )
        pl.semaphore_wait(barrier, len(everyone))

    def add(self, source, total, landing, base_of_landing):
        members = []
        for order, base, rows in self.mesh2.cut(total.shape[0]):
            i = len(self.streams)
            self.streams.append(
                dict(
                    source=source, total=total, landing=landing, base=base, land=base_of_landing + base, rows=rows,
                    order=order, own=self.own_rows, step=0,
                )
            )
            self.own_rows += rows >> self.bits
            members.append(i)
            self.send(i, 0)
        return members

    def kept(self, stream, t):
        if t == 0:
            return stream["source"], stream["base"]
        return stream["landing"], stream["land"] + stream["rows"] - (stream["rows"] >> (t - 1))

    def off(self, stream, t):
        at = stream["base"]
        for level in range(t):
            at = at + self.bit(*stream["order"][level]) * (stream["rows"] >> (level + 1))
        return pl.multiple_of(at, 16)

    def copy(self, i, t):
        stream = self.streams[i]
        if t < self.bits:
            axis, stride = stream["order"][t]
            half = stream["rows"] >> (t + 1)
            src, at = self.kept(stream, t)
            dst, landed = self.kept(stream, t + 1)
            src = src.at[pl.ds(pl.multiple_of(at + (1 - self.bit(axis, stride)) * half, 16), half), :]
            dst = dst.at[pl.ds(landed, half), :]
        else:
            level = 2 * self.bits - 1 - t
            axis, stride = stream["order"][level]
            size = stream["rows"] >> (level + 1)
            src = dst = stream["total"].at[pl.ds(self.off(stream, level + 1), size), :]
            if t == self.bits:
                src = self.own.at[pl.ds(stream["own"], size), :]
        return pltpu.make_async_remote_copy(
            src_ref=src,
            dst_ref=dst,
            send_sem=self.send_sem.at[i],
            recv_sem=self.recv_sem.at[i, t],
            device_id=self.partner(axis, stride),
            device_id_type=pl.DeviceIdType.MESH,
        )

    def keep_own(self, i):
        stream = self.streams[i]
        size = stream["rows"] >> self.bits
        return pltpu.make_async_copy(
            self.own.at[pl.ds(stream["own"], size), :],
            stream["total"].at[pl.ds(self.off(stream, self.bits), size), :],
            self.local_sem.at[i],
        )

    def send(self, i, t):
        stream = self.streams[i]
        self.copy(i, t).start()
        level = t if t < self.bits else 2 * self.bits - 1 - t
        size = (stream["rows"] >> (level + 1)) * PANEL * 2
        links = self.mesh2.links(*stream["order"][level])
        start = max([self.clock] + [self.free.get(link, 0.0) for link, _ in links])
        end = start
        for link, times in links:
            self.free[link] = start + times * size / (self.ICI if link else self.CORE)
            end = max(end, self.free[link])
        self.queue.append((end + self.LATENCY, i, t))

    def event(self, i, t):
        stream = self.streams[i]
        copy = self.copy(i, t)
        copy.wait_recv()
        if t < self.bits:
            axis, stride = stream["order"][t]
            half = stream["rows"] >> (t + 1)
            src, at = self.kept(stream, t)
            own = at + self.bit(axis, stride) * half
            landing, landed = self.kept(stream, t + 1)
            last = t + 1 == self.bits
            dst, to = (self.own, stream["own"]) if last else (landing, landed)
            tile = next(v for v in (128, 64, 32, 16) if half % v == 0)

            def add(k, carry):
                mine = src[pl.ds(pl.multiple_of(own + k * tile, 16), tile), :]
                other = landing[pl.ds(pl.multiple_of(landed + k * tile, 16), tile), :]
                dst[pl.ds(pl.multiple_of(to + k * tile, 16), tile), :] = mine + other
                return carry

            lax.fori_loop(0, half // tile, add, 0)
            if last:
                self.keep_own(i).start()
        if t == self.bits:
            self.keep_own(i).wait()
        copy.wait_send()
        stream["step"] = t + 1
        if t + 1 < 2 * self.bits:
            self.send(i, t + 1)

    def next(self):
        when, i, t = min(self.queue)
        self.queue.remove((when, i, t))
        self.clock = max(self.clock, when)
        self.event(i, t)

    def tick(self, cost):
        goal = self.clock + cost
        while self.queue and min(self.queue)[0] <= goal:
            self.next()
        self.clock = goal

    def until_sent(self, members):
        while any(self.streams[i]["step"] == 0 for i in members):
            self.next()

    def drain(self):
        while self.queue:
            self.next()


def stage(share, crop, ins, scratch, body):
    count = len(ins)

    def inner(*refs):
        loaded, sems, work = refs[:count], refs[count], refs[count + 1 :]
        copies = [pltpu.make_async_copy(a, b, sems.at[i]) for i, (a, b) in enumerate(zip(ins, loaded))]
        for copy in copies:
            copy.start()
        share.tick(1.5)
        for copy in copies:
            copy.wait()
        body(loaded, work)

    pl.run_scoped(
        inner,
        *[pltpu.VMEM(ref.shape, ref.dtype) for ref in ins],
        pltpu.SemaphoreType.DMA((count,)),
        *[pltpu.VMEM(shape, dtype) for shape, dtype in scratch],
    )


def backward_kernel(mesh2, rows, counts, crop, ids, *refs):
    groups, at = [], 0
    for count in counts:
        groups.append(refs[at : at + count])
        at += count
    box_in, cross_in, tag_in, feed_in, att_in, front_in, (boxes, dfeat), totals = groups
    source_0, source_a, source_b, landing, own, small, dt, dm, dh, local_sem, send_sem, recv_sem = refs[at:]
    n, width = dm.shape
    count = dt.shape[0]
    hidden = feed_in[3].shape[1]
    share = Share(mesh2, rows, own, local_sem, send_sem, recv_sem)
    tick = share.tick
    share.enter()
    lands = [sum(rows[:i]) for i in range(len(rows))]

    def begin(i, src):
        return share.add(src, totals[i], landing, lands[i])

    parts, at = [], 0
    for size in (24, 8, 72, 16, 8, 8):
        parts.append(small.at[at : at + size, :])
        at += size
    small[at:, :] = jnp.zeros((small.shape[0] - at, PANEL), F32)
    feeds = [None, None]

    def attend_scratch(queries, keys, times):
        return [((n, PANEL), F32)] + [
            ((queries, width), BF16), ((queries, width), BF16), ((width, queries), BF16), ((width, queries), BF16),
            ((width, keys), BF16), ((keys, times * width), BF16), ((width, queries), BF16),
            ((keys, queries), BF16), ((keys, queries), BF16),
        ]

    def box(loaded, work):
        def box_done():
            begin(0, source_0)

        box_kernel(crop, *loaded, boxes, dt, dm, source_0, source_b, parts[0], *work, box_done=box_done, tick=tick)

    tall, cell_count = (count, width), boxes.shape[1]
    stage(
        share, crop, box_in,
        [(tall, BF16), ((count, hidden), BF16), ((count, hidden), BF16), (tall, BF16), ((count, 1), F32), (tall, F32),
         ((count, hidden), BF16), (tall, F32), ((512, count), BF16), (tall, F32), (tall, BF16),
         ((cell_count, count), BF16), ((count, cell_count), BF16), ((cell_count, width), F32), ((cell_count, width), F32),
         ((1, n), F32), ((cell_count, n), F32), ((n, 2 * width), BF16), ((width, n), BF16)],
        box,
    )
    feeds[1] = begin(1, source_b)

    def cross(loaded, work):
        cross_backward_kernel(
            crop, dt, dm, *loaded, dt, dm, source_a, parts[1], work[0], dt, *work[1:], tick=tick
        )

    stage(share, crop, cross_in, attend_scratch(count, n, 2) + [((width, n), BF16)], cross)
    feeds[0] = begin(2, source_a)
    share.until_sent(feeds[1])

    def tags(loaded, work):
        tag_backward_kernel(
            dt, *loaded[:9], ids, *loaded[9:], source_b, parts[2], work[0], dt, *work[1:], tick=tick
        )

    stage(share, crop, tag_in, attend_scratch(count, count, 3), tags)
    feeds[1] = begin(3, source_b)
    share.until_sent(feeds[0])

    def feed(loaded, work):
        encoder_feed_backward_kernel(dm, *loaded, dh, source_a, parts[3], *work, tick=tick)

    stage(share, crop, feed_in, [((n, width), BF16), ((n, hidden), BF16), ((n, width), F32), ((512, n), BF16)], feed)
    feeds[0] = begin(4, source_a)
    share.until_sent(feeds[1])

    def attention(loaded, work):
        encoder_attention_backward_kernel(
            crop, dh, *loaded, dm, source_b, parts[4], work[0], work[1], *work[2:], tick=tick
        )

    scratch = attend_scratch(n, n, 3)
    stage(share, crop, att_in, scratch[:1] + [((n, width), BF16)] + scratch[1:], attention)
    feeds[1] = begin(5, source_b)
    share.until_sent(feeds[0])

    def front(loaded, work):
        feat, y1 = loaded[0], loaded[1]
        channels = y1.shape[1]

        def done_a():
            feeds[0] = begin(6, source_a)
            share.until_sent(feeds[1])

        def done_b():
            at = 9 * channels
            source_b[at : at + small.shape[0], :] = small[...].astype(BF16)
            begin(7, source_b)

        front_backward(
            crop, dm, *loaded, dfeat, source_a, source_b, parts[5], done_a, done_b, *work, tick=tick
        )

    channels = front_in[1].shape[1]
    stage(
        share, crop, front_in,
        [((n, width), BF16), ((n, channels), F32), ((n, channels), F32), ((n, channels), F32), (front_in[0].shape, F32),
         ((n + 64, 768), BF16), ((n + 64, channels), BF16)],
        front,
    )
    share.drain()


def cost_of(us):
    return pl.CostEstimate(flops=int(us * 1.1e9), bytes_accessed=int(us * 3.6e6), transcendentals=0)


def run(name, body, ins, outs, scratch, smem=0, us=10.0):
    shapes = [jax.ShapeDtypeStruct(shape, dtype) for shape, dtype in outs]
    fetched = ins[smem:]
    counts = [smem, len(fetched), len(outs), len(fetched), len(outs), len(scratch)]

    def whole(*refs):
        groups, at = [], 0
        for count in counts:
            groups.append(refs[at : at + count])
            at += count
        scalars, sources, targets, in_refs, out_refs, work = groups
        in_sem, out_sem = refs[at:]
        def load(i):
            return pltpu.make_async_copy(sources[i], in_refs[i], in_sem.at[i])

        def store(i):
            return pltpu.make_async_copy(out_refs[i], targets[i], out_sem.at[i])

        for i in range(len(in_refs)):
            load(i).start()
        here, gone = set(), set()

        def need(*wanted):
            for i, ref in enumerate(in_refs):
                if i not in here and any(ref is other for other in wanted):
                    load(i).wait()
                    here.add(i)

        def done(*ready):
            for i, ref in enumerate(out_refs):
                if i not in gone and any(ref is other for other in ready):
                    store(i).start()
                    gone.add(i)

        body(*scalars, *in_refs, *out_refs, *work, need=need, done=done)
        need(*in_refs)
        done(*out_refs)
        for i in range(len(out_refs)):
            store(i).wait()

    return pl.pallas_call(
        whole,
        out_shape=shapes,
        in_specs=[pl.BlockSpec(memory_space=pltpu.SMEM if i < smem else pltpu.HBM) for i in range(len(ins))],
        out_specs=[pl.BlockSpec(memory_space=pltpu.HBM)] * len(outs),
        scratch_shapes=[pltpu.VMEM(v.shape, v.dtype) for v in fetched]
        + [pltpu.VMEM(v.shape, v.dtype) for v in shapes]
        + [pltpu.VMEM(shape, dtype) for shape, dtype in scratch]
        + [pltpu.SemaphoreType.DMA((len(fetched),)), pltpu.SemaphoreType.DMA((len(outs),))],
        compiler_params=pltpu.CompilerParams(vmem_limit_bytes=VMEM_LIMIT),
        cost_estimate=cost_of(us),
        name=name,
    )(*ins)


def position_rows(count, width):
    places = np.arange(count, dtype=np.float32)[:, None]
    factor = np.exp(np.arange(width // 2, dtype=np.float32) * np.float32(-2.0 * math.log(10000.0) / width))
    angles = (places * factor.astype(np.float32)[None, :]).astype(np.float32)
    return np.concatenate([np.sin(angles), np.cos(angles)], axis=1).astype(np.float32)


def unpack_kernel(plan, small_plan, pack_count, *refs):
    packs = refs[:pack_count]
    out_count = len(plan) + len(small_plan)
    outs = refs[pack_count : pack_count + out_count]
    buffers = refs[pack_count + out_count : pack_count + out_count + pack_count]
    stages = refs[pack_count + out_count + pack_count : -2]
    in_sem, out_sem = refs[-2:]
    loads = [
        pltpu.make_async_copy(pack, buffer, in_sem.at[i]) for i, (pack, buffer) in enumerate(zip(packs, buffers))
    ]
    for load in loads:
        load.start()
    stores = []
    ready = set()
    for i, (group, base, rows, panels) in enumerate(plan):
        if group not in ready:
            loads[group].wait()
            ready.add(group)
        for c in range(panels):
            stages[i][:, c * PANEL : (c + 1) * PANEL] = buffers[group][base + c * rows : base + (c + 1) * rows, :].astype(F32)
        store = pltpu.make_async_copy(stages[i], outs[i], out_sem.at[i])
        store.start()
        stores.append(store)
    if pack_count - 1 not in ready:
        loads[-1].wait()
    for k, pieces in enumerate(small_plan):
        i = len(plan) + k
        for to, base, rows, width in pieces:
            start = base // 16 * 16
            stop = -(-(base + rows * width // PANEL) // 16) * 16
            block = buffers[-1][start:stop, :].astype(F32)
            for c in range(width // PANEL):
                at = base - start + c * rows
                stages[i][to : to + rows, c * PANEL : (c + 1) * PANEL] = block[at : at + rows, :]
        store = pltpu.make_async_copy(stages[i], outs[i], out_sem.at[i])
        store.start()
        stores.append(store)
    for store in stores:
        store.wait()


def train(mesh2, features, crop_side, tag_ids, tag_count, cell_pick, box_units, weights):
    (
        conv_first, conv_first_bias, conv_second, conv_second_bias, projection, projection_bias,
        encoder_attention, encoder_output, attention_gain, attention_shift,
        encoder_up, encoder_up_bias, encoder_down, encoder_down_bias, feedforward_gain, feedforward_shift,
        tag_table, decoder_attention, decoder_output, decoder_query, decoder_memory, decoder_cross,
        decoder_up, decoder_up_bias, decoder_down, decoder_down_bias, decoder_gain, decoder_shift,
        box_query, box_memory, box_output, box_hidden, box_hidden_bias, box_coord,
    ) = weights
    feature_map = features[0, 0]
    n = GRID * PITCH
    cells_in, channels = feature_map.shape
    width = projection.shape[1]
    hidden = encoder_up.shape[1]
    count = tag_ids.shape[2]
    cell_count = cell_pick.shape[2]
    vocab = tag_table.shape[0]

    def row(v):
        return v.reshape(1, -1)

    def packed(rows):
        return ((mesh2.padded(rows), PANEL), BF16)

    cell_positions = np.zeros((GRID, PITCH, width), np.float32)
    cell_positions[:, :GRID] = position_rows(GRID * GRID, width).reshape(GRID, GRID, width)
    cell_positions = jnp.asarray(cell_positions.reshape(n, width))
    tag_positions = jnp.asarray(position_rows(count, width))

    big, tall = (n, width), (count, width)
    stats = [((width, n), F32), ((HEADS, 1, n), F32), (big, BF16), ((n, 1), F32)]
    tag_stats = [((width, count), F32), ((HEADS, 1, count), F32), (tall, BF16), ((count, 1), F32)]
    ins = [
        [feature_map, conv_first, row(conv_first_bias), conv_second, row(conv_second_bias), projection, row(projection_bias),
         cell_positions],
        [encoder_attention, encoder_output, row(attention_gain), row(attention_shift)],
        [encoder_up, row(encoder_up_bias), encoder_down, row(encoder_down_bias), row(feedforward_gain),
         row(feedforward_shift), decoder_memory, box_memory],
        [tag_ids, tag_table, tag_positions, decoder_attention, decoder_output, decoder_gain, decoder_shift],
        [decoder_query, decoder_cross],
    ]
    outs = [
        [((n, channels), BF16)] * 4,
        [(big, BF16)] * 4 + stats + [(big, BF16)],
        [((n, hidden), BF16)] * 2 + [(big, BF16), ((n, 1), F32), (big, BF16)] + [((n, 2 * width), BF16)] * 2,
        [(tall, BF16)] * 4 + tag_stats,
        [(tall, BF16)] * 2 + tag_stats + [(tall, F32)],
    ]
    (
        y1, g1, y2, g2,
        eb, eq, ek, ev, eo, else_, en, ei, h,
        u, gu, fn, fi, memory, pairs, box_pairs,
        t0b, tq, tk, tv, to, tlse, tn, ti,
        t1b, cq, co, clse, cn, ci, t2,
    ) = run(
        "forward", functools.partial(forward_kernel, [len(g) for g in ins] + [len(g) for g in outs]),
        [crop_side] + [v for g in ins for v in g], [v for g in outs for v in g], [(big, F32), (tall, F32)], 1, us=80.0,
    )
    up_rows = width * hidden // PANEL
    sq_rows = width * width // PANEL
    coord16 = jnp.pad(box_coord.T, ((0, 12), (0, 0)))
    conv_rows = 9 * channels
    groups = [
        [tag_count, t2, decoder_up, row(decoder_up_bias), decoder_down, row(decoder_down_bias), decoder_gain,
         decoder_shift, cell_pick, box_units, box_pairs, memory,
         box_query, box_memory, box_output, box_hidden, row(box_hidden_bias), coord16],
        [cn, ci, decoder_gain, co, clse, cq, pairs, t1b, memory, decoder_query, decoder_memory, decoder_cross],
        [tn, ti, decoder_gain, to, tlse, tq, tk, tv, t0b, decoder_attention, decoder_output],
        [fn, fi, row(feedforward_gain), u, gu, h, encoder_up, encoder_down],
        [en, ei, row(attention_gain), eo, else_, eq, ek, ev, eb, encoder_attention, encoder_output],
        [feature_map, y1, g1, y2, g2, conv_first, conv_second, projection],
    ]
    small_rows = 144
    rows = [5 * sq_rows, 2 * up_rows, 4 * sq_rows, 4 * sq_rows, 2 * up_rows, 4 * sq_rows, 2 * channels + conv_rows, conv_rows + small_rows]
    rows = [mesh2.padded(r) for r in rows]
    streams = sum(len(mesh2.cut(r)) for r in rows)
    bits = len(mesh2.core + mesh2.rest)
    flat = [v for group in groups for v in group]
    spaces = [pltpu.SMEM, pltpu.VMEM] + [pl.ANY] * len(flat)
    boxes, dfeat, *packs = pl.pallas_call(
        functools.partial(backward_kernel, mesh2, rows, [len(g) for g in groups] + [2, len(rows)]),
        out_shape=[jax.ShapeDtypeStruct((4, cell_count), F32), jax.ShapeDtypeStruct((cells_in, channels), BF16)] + [jax.ShapeDtypeStruct((r, PANEL), BF16) for r in rows],
        in_specs=[pl.BlockSpec(memory_space=space) for space in spaces],
        out_specs=[pl.BlockSpec(memory_space=pltpu.VMEM)] * 2 + [pl.BlockSpec(memory_space=pl.ANY)] * len(rows),
        scratch_shapes=[
            pltpu.VMEM((rows[0], PANEL), BF16),
            pltpu.VMEM((max(rows[1:]), PANEL), BF16),
            pltpu.VMEM((max(rows[1:]), PANEL), BF16),
            pltpu.VMEM((sum(rows), PANEL), BF16),
            pltpu.VMEM((sum(rows) // mesh2.devices, PANEL), BF16),
            pltpu.VMEM((small_rows, PANEL), F32),
            pltpu.VMEM(tall, F32), pltpu.VMEM(big, F32), pltpu.VMEM(big, F32),
            pltpu.SemaphoreType.DMA((streams,)),
            pltpu.SemaphoreType.DMA((streams,)),
            pltpu.SemaphoreType.DMA((streams, 2 * bits)),
        ],
        compiler_params=pltpu.CompilerParams(vmem_limit_bytes=VMEM_LIMIT, collective_id=1, has_side_effects=True),
        cost_estimate=cost_of(180.0),
        name="backward",
    )(crop_side, tag_ids, *flat)
    plan = {
        31: (0, 0, width, 2), 30: (0, sq_rows, width, 2), 28: (0, 2 * sq_rows, width, 2), 29: (0, 3 * sq_rows, width, 4),
        22: (1, 0, width, hidden // PANEL), 24: (1, up_rows, hidden, 2),
        21: (2, 0, width, 2), 19: (2, sq_rows, width, 2), 20: (2, 2 * sq_rows, width, 4),
        18: (3, 0, width, 2), 17: (3, sq_rows, width, 6),
        10: (4, 0, width, hidden // PANEL), 12: (4, up_rows, hidden, 2),
        7: (5, 0, width, 2), 6: (5, sq_rows, width, 6),
        4: (6, 0, channels, 2), 2: (6, 2 * channels, conv_rows, 1), 0: (7, 0, conv_rows, 1),
    }
    one, up = width // PANEL, hidden // PANEL
    at_box = conv_rows
    at_cross = at_box + 24
    at_tag = at_cross + 8
    at_feed = at_tag + 72
    at_att = at_feed + 16
    at_front = at_att + 8
    small_plan = {
        26: [(2, at_box, 1, width), (1, at_cross, 1, width), (0, at_tag, 1, width)],
        27: [(2, at_box + one, 1, width), (1, at_cross + one, 1, width), (0, at_tag + one, 1, width)],
        25: [(0, at_box + 2 * one, 1, width)], 23: [(0, at_box + 3 * one, 1, hidden)],
        32: [(0, at_box + 3 * one + up, 1, width)], 33: [(0, at_box + 4 * one + up, 4, width)],
        16: [(0, at_tag + 2 * one, vocab, width)],
        14: [(0, at_feed, 1, width)], 15: [(0, at_feed + one, 1, width)],
        13: [(0, at_feed + 2 * one, 1, width)], 11: [(0, at_feed + 3 * one, 1, hidden)],
        8: [(0, at_att, 1, width)], 9: [(0, at_att + one, 1, width)],
        5: [(0, at_front, 1, width)], 3: [(0, at_front + one, 1, channels)], 1: [(0, at_front + one + 1, 1, channels)],
    }
    shapes = [weights[k].shape for k in plan]
    shapes += [(sum(rows for _, _, rows, _ in pieces), pieces[0][3]) for pieces in small_plan.values()]
    outs = pl.pallas_call(
        functools.partial(unpack_kernel, list(plan.values()), list(small_plan.values()), len(packs)),
        out_shape=[jax.ShapeDtypeStruct(shape, F32) for shape in shapes],
        in_specs=[pl.BlockSpec(memory_space=pl.ANY)] * len(packs),
        out_specs=[pl.BlockSpec(memory_space=pl.ANY)] * len(shapes),
        scratch_shapes=[pltpu.VMEM(p.shape, BF16) for p in packs]
        + [pltpu.VMEM(shape, F32) for shape in shapes]
        + [pltpu.SemaphoreType.DMA((len(packs),)), pltpu.SemaphoreType.DMA((len(shapes),))],
        compiler_params=pltpu.CompilerParams(vmem_limit_bytes=VMEM_LIMIT),
        name="unpack",
    )(*packs)
    found = dict(zip(list(plan) + list(small_plan), outs))
    found[33] = found[33].T
    result = [found[k].reshape(weight.shape) for k, weight in enumerate(weights)]
    return tuple([boxes[None, None], dfeat[None, None]] + result)


def solution(mesh):
    mesh2 = Mesh2(mesh.shape[SECTION], mesh.shape[SPLIT])

    def local(features, crop_side, tag_ids, tag_count, cell_pick, box_units, *weights):
        return train(mesh2, features, crop_side, tag_ids, tag_count, cell_pick, box_units, weights)

    in_specs = (
        P(SECTION, SPLIT, None, None), P(), P(None, SPLIT, None), P(None, SPLIT), P(None, SPLIT, None),
        P(None, SPLIT, None, None),
    ) + (P(),) * 34
    out_specs = (P(SECTION, SPLIT, None, None),) * 2 + (P(),) * 34
    return jax.shard_map(local, mesh=mesh, in_specs=in_specs, out_specs=out_specs, check_vma=False)
```

```python
import functools
import math

import jax
import jax.numpy as jnp
import numpy as np
from jax import lax
from jax.experimental import pallas as pl
from jax.experimental.pallas import tpu as pltpu
from jax.sharding import PartitionSpec as P

HEADS = 8
GRID = 28
PITCH = 32
F32 = jnp.float32
BF16 = jnp.bfloat16
NEG = -1e30
SECTION = "section"
SPLIT = "dp"
PANEL = 256
VMEM_LIMIT = 60 * 1024 * 1024


def mm(a, b):
    return jnp.dot(a, b, preferred_element_type=F32)


def mm_nt(a, b):
    return lax.dot_general(a, b, (((1,), (1,)), ((), ())), preferred_element_type=F32)


def rows_loop(total, tile, body):
    def step(i, carry):
        body(pl.ds(pl.multiple_of(i * tile, tile), tile))
        return carry

    lax.fori_loop(0, total // tile, step, 0)


def rows_sum(total, tile, width, body, count=1):
    def step(i, carry):
        parts = body(pl.ds(pl.multiple_of(i * tile, tile), tile))
        return tuple(c + part for c, part in zip(carry, parts))

    zeros = tuple(jnp.zeros((8, width), F32) for _ in range(count))
    sums = lax.fori_loop(0, total // tile, step, zeros)
    return tuple(jnp.sum(s, axis=0, keepdims=True) for s in sums)


def eights(v):
    return jnp.sum(v.reshape(v.shape[0] // 8, 8, v.shape[1]), axis=0)


def gelu_pair(z):
    phi = 0.5 * (1.0 + lax.erf(z * 0.7071067811865476))
    bell = jnp.exp(z * z * -0.5) * 0.3989422804014327
    return z * phi, phi + z * bell


def inside_rows(start, rows, width, side):
    cell = lax.broadcasted_iota(jnp.int32, (rows, width), 0) + start
    return ((cell >> 5) < side) & ((cell & 31) < side)


def norm_forward(v, gain, shift):
    centre = v - jnp.mean(v, axis=-1, keepdims=True)
    spread = jnp.mean(centre * centre, axis=-1, keepdims=True)
    inv = lax.rsqrt(spread + 1e-05)
    normal = centre * inv
    return normal, inv, normal * gain + shift


def norm_backward(dy, normal, inv, gain):
    d = dy * gain
    return (
        d
        - jnp.mean(d, axis=-1, keepdims=True)
        - normal * jnp.mean(d * normal, axis=-1, keepdims=True)
    ) * inv


def no_tick(cost):
    pass


def put_panels(out, base, left, right, tick=no_tick, cost=0.0):
    rows = left.shape[0]
    panels = right.shape[1] // PANEL
    for c in range(panels):
        value = mm(left[...], right[:, c * PANEL : (c + 1) * PANEL])
        out[base + c * rows : base + (c + 1) * rows, :] = value.astype(BF16)
        tick(cost / panels)


def put_small(out, at, value):
    for c in range(value.shape[1] // PANEL):
        rows = value.shape[0]
        out[at + c * rows : at + (c + 1) * rows, :] = value[:, c * PANEL : (c + 1) * PANEL]
    return at + value.shape[0] * value.shape[1] // PANEL


def put_smalls(out, at, values):
    for value in values:
        at = put_small(out, at, value)
    return at


def lane_tiles(total):
    return [(s, min(256, total - s)) for s in range(0, total, 256)]


CHUNK = 128


def folded(v, how):
    return how(v.reshape(v.shape[0] // 8, 8, v.shape[1]), axis=0)


def scores_of(key_part, query_part, mask, causal, at, start, size):
    s = mm(key_part, query_part)
    if not causal:
        return s + mask[at : at + CHUNK, :size]
    if at + CHUNK <= start:
        return s
    key_at = lax.broadcasted_iota(jnp.int32, (CHUNK, size), 0) + at
    query_at = lax.broadcasted_iota(jnp.int32, (CHUNK, size), 1) + start
    return jnp.where(key_at <= query_at, s, NEG)


def attend_forward(keys, q_t, v_t, out_t, lse, mask, causal, s_s, w_s):
    key_count = keys.shape[0]

    def pair(hp, carry):
        lanes = pl.ds(pl.multiple_of(hp * 128, 128), 128)
        for j in range(2):
            rows = pl.ds(pl.multiple_of(hp * 128 + 64 * j, 64), 64)
            for start, size in lane_tiles(q_t.shape[1]):
                seen = min(start + size, key_count) if causal else key_count
                query_part = q_t[rows, start : start + size]
                top = None
                for at in range(0, seen, CHUNK):
                    key_part = keys[at : at + CHUNK, lanes][:, 64 * j : 64 * j + 64]
                    s = scores_of(key_part, query_part, mask, causal, at, start, size)
                    s_s[at : at + CHUNK, :size] = s
                    part = folded(s, jnp.max)
                    top = part if top is None else jnp.maximum(top, part)
                top = jnp.max(top, axis=0, keepdims=True)
                total = jnp.zeros((8, size), F32)
                for at in range(0, seen, CHUNK):
                    w = jnp.exp(s_s[at : at + CHUNK, :size] - top)
                    total = total + folded(w, jnp.sum)
                    w_s[at : at + CHUNK, :size] = w.astype(BF16)
                total = jnp.sum(total, axis=0, keepdims=True)
                out_t[rows, start : start + size] = mm(v_t[rows, :seen], w_s[:seen, :size]) / total
                lse[2 * hp + j, :, start : start + size] = top + jnp.log(total)
        return carry

    lax.fori_loop(0, HEADS // 2, pair, 0)


def attend_backward(keys, values, keys_t, q, q_t, do, do_t, out_t, lse, mask, causal, dk, dv, dq_t, p_s, ds_s, tick, cost):
    key_count = keys.shape[0]
    share = cost / (HEADS * (len(lane_tiles(q_t.shape[1])) + 1))

    for hp in range(HEADS // 2):
        lanes = slice(hp * 128, hp * 128 + 128)
        q_pair = q[:, lanes]
        do_pair = do[:, lanes]
        dks = []
        dvs = []
        for j in range(2):
            rows = slice(hp * 128 + 64 * j, hp * 128 + 64 * j + 64)
            part = slice(64 * j, 64 * j + 64)
            for start, size in lane_tiles(q_t.shape[1]):
                cols = slice(start, start + size)
                seen = min(start + size, key_count) if causal else key_count
                query_part = q_t[rows, cols]
                do_part = do_t[rows, cols]
                log_total = lse[2 * hp + j, :, cols]
                dsum = jnp.sum(do_part.astype(F32) * out_t[rows, cols], axis=0, keepdims=True)
                for at in range(0, seen, CHUNK):
                    chunk = slice(at, at + CHUNK)
                    s = scores_of(keys[chunk, lanes][:, part], query_part, mask, causal, at, start, size)
                    p = jnp.exp(s - log_total)
                    p_s[chunk, cols] = p.astype(BF16)
                    dp = mm(values[chunk, lanes][:, part], do_part)
                    ds_s[chunk, cols] = (p * (dp - dsum)).astype(BF16)
                if causal and seen < key_count:
                    p_s[seen:, cols] = jnp.zeros((key_count - seen, size), BF16)
                    ds_s[seen:, cols] = jnp.zeros((key_count - seen, size), BF16)
                dq_t[rows, cols] = (mm(keys_t[rows, :seen], ds_s[:seen, cols]) * 0.125).astype(BF16)
                tick(share)
            dks.append(mm(ds_s[...], q_pair[:, part]))
            dvs.append(mm(p_s[...], do_pair[:, part]))
            tick(share)
        dk[:, lanes] = jnp.concatenate(dks, axis=1).astype(BF16)
        dv[:, lanes] = jnp.concatenate(dvs, axis=1).astype(BF16)


def im2col(value, dst):
    n = value.shape[0]
    blank = jnp.zeros((PITCH, 3 * PANEL), BF16)
    dst[0:PITCH, :] = blank
    dst[n + PITCH : n + 2 * PITCH, :] = blank
    dst[PITCH : n + PITCH, 0:PANEL] = pltpu.roll(value, 1, 0).astype(BF16)
    dst[PITCH : n + PITCH, PANEL : 2 * PANEL] = value.astype(BF16)
    dst[PITCH : n + PITCH, 2 * PANEL :] = pltpu.roll(value, n - 1, 0).astype(BF16)


def conv_of(cols, w, n):
    return (
        mm(cols[0:n, :], w[0:768, :])
        + mm(cols[PITCH : n + PITCH, :], w[768:1536, :])
        + mm(cols[2 * PITCH : n + 2 * PITCH, :], w[1536:2304, :])
    )


def front_kernel(crop, feat, w1, b1, w2, b2, wp, bp, pos, e, y1, g1, y2, g2, wide, x, z, cols, need, done):
    n = x.shape[0]
    need(feat)
    wide[...] = feat[...].astype(F32)
    x[...] = jnp.zeros_like(x)
    for r in range(GRID):
        x[r * PITCH : r * PITCH + GRID, :] = wide[r * GRID : (r + 1) * GRID, :]
    s = own_side(crop)
    x[...] = jnp.where(inside_rows(0, n, PANEL, s), x[...], 0.0)
    im2col(x[...], cols)
    need(w1, b1)
    z[...] = conv_of(cols, w1, n)

    def first(rows):
        y, g = gelu_pair(z[rows, :] + b1[...])
        ins = inside_rows(rows.start, rows.size, PANEL, s)
        y = jnp.where(ins, y, 0.0)
        z[rows, :] = y
        y1[rows, :] = y.astype(BF16)
        g1[rows, :] = jnp.where(ins, g, 0.0).astype(BF16)

    rows_loop(n, 64, first)
    done(y1, g1)
    im2col(z[...], cols)
    need(w2, b2)
    z[...] = conv_of(cols, w2, n)

    def second(rows):
        y, g = gelu_pair(z[rows, :] + b2[...] + x[rows, :])
        ins = inside_rows(rows.start, rows.size, PANEL, s)
        y2[rows, :] = jnp.where(ins, y, 0.0).astype(BF16)
        g2[rows, :] = jnp.where(ins, g, 0.0).astype(BF16)

    rows_loop(n, 64, second)
    done(y2, g2)
    need(wp, bp, pos)
    for c in range(2):
        cut = slice(c * PANEL, (c + 1) * PANEL)
        e[:, cut] = mm(y2[...], wp[:, cut]) + bp[:, cut] + pos[:, cut]


def own_side(crop):
    return crop[lax.axis_index(SECTION)]


def fill_mask(mask, crop):
    n = mask.shape[0]
    side = own_side(crop)
    mask[...] = jnp.where(inside_rows(0, n, PANEL, side), 0.0, NEG)


def split_qkv(x, w, keys, q, q_t, v, v_t):
    for c in range(2):
        cut = slice(c * PANEL, (c + 1) * PANEL)
        part = (mm(x[...], w[:, c * PANEL : (c + 1) * PANEL]).astype(BF16) * 0.125).astype(BF16)
        q[:, cut] = part
        q_t[cut, :] = part.T
        keys[:, cut] = mm(x[...], w[:, 512 + c * PANEL : 512 + (c + 1) * PANEL]).astype(BF16)
        part = mm(x[...], w[:, 1024 + c * PANEL : 1024 + (c + 1) * PANEL]).astype(BF16)
        v[:, cut] = part
        v_t[cut, :] = part.T


def self_forward(xb, x, w, wo, gain, shift, q, keys, v, out_t, lse, normal, inv, h, mask, causal, q_t, v_t, z, s_s, w_s, need, done):
    need(w)
    split_qkv(xb, w, keys, q, q_t, v, v_t)
    done(xb, q, keys, v)
    attend_forward(keys, q_t, v_t, out_t, lse, mask, causal, s_s, w_s)
    done(out_t, lse)
    need(wo)
    z[...] = mm(out_t[...].astype(BF16).T, wo[...])

    def finish(rows):
        nn, ii, y = norm_forward(x[rows, :] + z[rows, :], gain[...], shift[...])
        normal[rows, :] = nn.astype(BF16)
        inv[rows, :] = ii
        h[rows, :] = y.astype(h.dtype)

    rows_loop(x.shape[0], 64, finish)


def encoder_attention_kernel(crop, e, w, wo, gain, shift, eb, q, keys, v, out_t, lse, normal, inv, h, mask, q_t, v_t, z, s_s, w_s, need, done):
    fill_mask(mask, crop)
    need(e, gain, shift)
    eb[...] = e[...].astype(BF16)
    self_forward(eb, e, w, wo, gain, shift, q, keys, v, out_t, lse, normal, inv, h, mask, False, q_t, v_t, z, s_s, w_s, need, done)


def encoder_feed_kernel(h, wu, bu, wd, bd, gain, shift, wm, wb, u, gu, normal, inv, memory, pairs, box_pairs, z, f, need, done):
    n = h.shape[0]
    need(h, wu, bu)
    for c in range(wu.shape[1] // 512):
        cut = slice(c * 512, (c + 1) * 512)
        z[...] = mm(h[...], wu[:, cut])

        def grow(rows):
            y, g = gelu_pair(z[rows, :] + bu[:, cut])
            u[rows, cut] = y.astype(BF16)
            gu[rows, cut] = g.astype(BF16)

        rows_loop(n, 64, grow)
    done(u, gu)
    need(wd, bd, gain, shift)
    f[...] = mm(u[...], wd[...])

    def finish(rows):
        nn, ii, y = norm_forward(h[rows, :].astype(F32) + f[rows, :] + bd[...], gain[...], shift[...])
        normal[rows, :] = nn.astype(BF16)
        inv[rows, :] = ii
        memory[rows, :] = y.astype(BF16)

    rows_loop(n, 64, finish)
    done(normal, inv, memory)
    need(wm)
    for c in range(2):
        cut = slice(c * 512, (c + 1) * 512)
        pairs[:, cut] = mm(memory[...], wm[:, cut]).astype(BF16)
    done(pairs)
    need(wb)
    for c in range(2):
        cut = slice(c * 512, (c + 1) * 512)
        box_pairs[:, cut] = mm(memory[...], wb[:, cut]).astype(BF16)


def hot_columns(row, rows):
    return (row == lax.broadcasted_iota(jnp.int32, (rows, row.shape[1]), 0)).astype(F32)


def tag_kernel(ids, table, pos, w, wo, gain, shift, t0b, q, keys, v, out_t, lse, normal, inv, t1, mask, q_t, v_t, z, s_s, w_s, t0, need, done):
    need(ids, table, pos, gain, shift)
    hot = hot_columns(ids[lax.axis_index(SECTION)], table.shape[0])
    t0[...] = mm(hot.T.astype(BF16), table[...]) + pos[...]
    t0b[...] = t0[...].astype(BF16)
    self_forward(t0b, t0, w, wo, gain.at[0:1, :], shift.at[0:1, :], q, keys, v, out_t, lse, normal, inv, t1, mask, True, q_t, v_t, z, s_s, w_s, need, done)


def cross_kernel(crop, t1, pairs, wq, wo, gain, shift, t1b, q, out_t, lse, normal, inv, t2, mask, q_t, v_t, z, s_s, w_s, need, done):
    fill_mask(mask, crop)
    need(t1, wq, gain, shift)
    t1b[...] = t1[...].astype(BF16)
    part = (mm(t1b[...], wq[...]).astype(BF16) * 0.125).astype(BF16)
    q[...] = part
    q_t[...] = part.T
    need(pairs)
    v_t[...] = pairs[:, 512:].T
    done(t1b, q)
    attend_forward(pairs, q_t, v_t, out_t, lse, mask, False, s_s, w_s)
    done(out_t, lse)
    need(wo)
    z[...] = mm(out_t[...].astype(BF16).T, wo[...])

    def finish(rows):
        nn, ii, y = norm_forward(t1[rows, :] + z[rows, :], gain[1:2, :], shift[1:2, :])
        normal[rows, :] = nn.astype(BF16)
        inv[rows, :] = ii
        t2[rows, :] = y

    rows_loop(t1.shape[0], 64, finish)


def scoped(body, refs, scratch, need, done):
    pl.run_scoped(
        lambda *work: body(*refs, *work, need=need, done=done), *[pltpu.VMEM(shape, dtype) for shape, dtype in scratch]
    )


def forward_kernel(counts, crop, *refs, need, done):
    groups, at = [], 0
    for count in counts:
        groups.append(refs[at : at + count])
        at += count
    front_in, att_in, feed_in, tag_in, cross_in, front_out, att_out, feed_out, tag_out, cross_out = groups
    e, t1 = refs[at:]
    (n, width), count = e.shape, t1.shape[0]
    big, tall = (n, width), (count, width)
    cells_in, channels = front_in[0].shape
    scoped(
        front_kernel, (crop, *front_in, e, *front_out),
        [((cells_in, channels), F32), ((n, channels), F32), ((n, channels), F32), ((n + 64, 3 * channels), BF16)], need, done,
    )
    scoped(
        encoder_attention_kernel, (crop, e, *att_in, *att_out),
        [((n, PANEL), F32), ((width, n), BF16), ((width, n), BF16), (big, F32), ((n, PANEL), F32), ((n, PANEL), BF16)], need, done,
    )
    h = att_out[-1]
    scoped(encoder_feed_kernel, (h, *feed_in, *feed_out), [(big, F32), (big, F32)], need, done)
    scoped(
        tag_kernel, (*tag_in, *tag_out, t1),
        [((8, 128), F32), ((width, count), BF16), ((width, count), BF16), (tall, F32), ((count, PANEL), F32), ((count, PANEL), BF16),
         (tall, F32)], need, done,
    )
    pairs, gain, shift = feed_out[-2], tag_in[-2], tag_in[-1]
    scoped(
        cross_kernel, (crop, t1, pairs, *cross_in, gain, shift, *cross_out),
        [((n, PANEL), F32), ((width, count), BF16), ((width, n), BF16), (tall, F32), ((n, PANEL), F32), ((n, PANEL), BF16)], need, done,
    )


def feed_backward(dy, dy_b, normal, inv, gain, u, gu, xb, wu, wd, g_up, g_down, small, dx_out, dz, dx, t_s, tick=no_tick):
    n, width = dy.shape

    def through(rows):
        d = dy[rows, :]
        nn = normal[rows, :].astype(F32)
        out = norm_backward(d, nn, inv[rows, :], gain[...])
        dx[rows, :] = out
        dy_b[rows, :] = out.astype(BF16)
        return eights(d * nn), eights(d), eights(out)

    at = put_smalls(small, 0, rows_sum(n, 64, width, through, 3))
    tick(1.5)
    for c in range(u.shape[1] // 512):
        cut = slice(c * 512, (c + 1) * 512)
        t_s[...] = u[:, cut].T
        for p in range(width // PANEL):
            value = mm(t_s[...], dy_b[:, p * PANEL : (p + 1) * PANEL])
            row = p * u.shape[1] + c * 512
            g_down[row : row + 512, :] = value.astype(BF16)
            tick(0.8)
        dx_out[...] = mm_nt(dy_b[...], wd[cut, :])
        tick(1.2)

        def narrow(rows):
            d = dx_out[rows, :] * gu[rows, cut].astype(F32)
            dz[rows, cut] = d.astype(BF16)
            return (eights(d),)

        at = put_small(small, at, rows_sum(n, 64, 512, narrow)[0])
        tick(0.6)
    t_s[...] = xb[...].T
    put_panels(g_up, 0, t_s, dz, tick, 3.0)
    dx_out[...] = dx[...] + mm_nt(dz[...], wu[...])
    tick(2.0)
    return at


def box_kernel(
    crop, totals, t2, wu, bu, wd, bd, gains, shifts, picks, units, pairs, memory, wq, wm, wo, wh, bh, wc_t,
    boxes, dt2, dmem, grads, ffn, small,
    t2b, u, gu, normal, inv, z, dz, dx, t_s, d3, db, hot, hot_t, cells, dcells, mask, p_s, dpairs, mem_t, box_done, tick,
):
    gain, shift = gains.at[2:3, :], shifts.at[2:3, :]
    section = lax.axis_index(SECTION)
    side = crop[section]
    count = t2.shape[0]
    t2b[...] = t2[...].astype(BF16)
    for c in range(wu.shape[1] // 512):
        cut = slice(c * 512, (c + 1) * 512)
        z[...] = mm(t2b[...], wu[:, cut])

        def grow(rows):
            y, g = gelu_pair(z[rows, :] + bu[:, cut])
            u[rows, cut] = y.astype(BF16)
            gu[rows, cut] = g.astype(BF16)

        rows_loop(count, 64, grow)
    z[...] = mm(u[...], wd[...])

    def finish(rows):
        nn, ii, y = norm_forward(t2[rows, :] + z[rows, :] + bd[...], gain[...], shift[...])
        normal[rows, :] = nn.astype(BF16)
        inv[rows, :] = ii
        d3[rows, :] = y

    rows_loop(count, 64, finish)
    place = (picks[section] * totals[pl.ds(section, 1), :]) >> 15
    hot_f = hot_columns(place, count)
    hot_t[...] = hot_f.astype(BF16)
    hot[...] = hot_f.T.astype(BF16)
    high = d3[...].astype(BF16)
    rest = (d3[...] - high.astype(F32)).astype(BF16)
    cells[...] = mm(hot[...], high) + mm(hot[...], rest)
    cells_b = cells[...].astype(BF16)
    queries = mm(cells_b, wq[...]).astype(BF16)
    scale = 512.0 ** (-0.5)
    cell = lax.broadcasted_iota(jnp.int32, mask.shape, 1)
    mask[...] = jnp.where(((cell >> 5) < side) & ((cell & 31) < side), 0.0, NEG)
    s = mm_nt(queries, pairs[:, :512]) * scale + mask[...]
    s = jnp.exp(s - jnp.max(s, axis=1, keepdims=True))
    p_s[...] = s / jnp.sum(s, axis=1, keepdims=True)
    p_b = p_s[...].astype(BF16)
    context = mm(p_b, pairs[:, 512:]).astype(BF16)
    enriched = cells[...] + mm(context, wo[...])
    enriched_b = enriched.astype(BF16)
    hidden, slope = gelu_pair(mm(enriched_b, wh[...]) + bh[...])
    hidden_b = hidden.astype(BF16)
    guess = 1.0 / (1.0 + jnp.exp(-mm_nt(wc_t[...], hidden_b)))
    boxes[...] = guess[0:4]
    guess = guess[0:4]
    missed = guess - units[section, 0].astype(F32) * (1.0 / 1024.0)
    dlogit = 4.0 * missed * lax.rsqrt(1.0 + 16.0 * missed * missed) * guess * (1.0 - guess)
    dlogit = jnp.concatenate([dlogit, jnp.zeros((12, dlogit.shape[1]), F32)], axis=0)
    dwc_t = mm(dlogit.astype(BF16), hidden_b)
    dhidden = mm(dlogit.T.astype(BF16), wc_t[...]) * slope
    dhidden_b = dhidden.astype(BF16)
    put_panels(grads, 0, enriched_b.T, dhidden_b)
    dcells[...] = mm_nt(dhidden_b, wh[...])
    dout_b = dcells[...].astype(BF16)
    put_panels(grads, 1024, context.T, dout_b)
    dcontext = mm_nt(dout_b, wo[...]).astype(BF16)
    dp = mm_nt(dcontext, pairs[:, 512:])
    p = p_s[...].astype(BF16).astype(F32)
    ds = (p * (dp - jnp.sum(dp * p, axis=1, keepdims=True))).astype(BF16)
    dqueries = (mm(ds, pairs[:, :512]) * scale).astype(BF16)
    dpairs[:, :512] = (mm(ds.T, queries) * scale).astype(BF16)
    dpairs[:, 512:] = mm(p_b.T, dcontext).astype(BF16)
    put_panels(grads, 2048, cells_b.T, dqueries)
    dcells[...] += mm_nt(dqueries, wq[...])
    mem_t[...] = memory[...].T
    put_panels(grads, 3072, mem_t, dpairs)
    box_done()
    dmem[...] = mm_nt(dpairs[...], wm[...])
    tick(1.0)
    high = dcells[...].astype(BF16)
    rest = (dcells[...] - high.astype(F32)).astype(BF16)
    d3[...] = mm(hot_t[...], high) + mm(hot_t[...], rest)
    up_rows = 512 * wu.shape[1] // PANEL
    small[...] = jnp.zeros_like(small)
    tick(0.6)
    at = feed_backward(
        d3, db, normal, inv, gain, u, gu, t2b, wu, wd,
        ffn.at[0:up_rows, :], ffn.at[up_rows : 2 * up_rows, :], small, dt2, dz, dx, t_s, lambda cost: tick(0.6 * cost),
    )
    put_smalls(small, at, (jnp.sum(dhidden, axis=0, keepdims=True), dwc_t[0:4]))


def norm_rows_backward(dy, normal, inv, gain, small, dx, dxb):
    def through(rows):
        d = dy[rows, :].astype(F32)
        nn = normal[rows, :].astype(F32)
        out = norm_backward(d, nn, inv[rows, :], gain[...])
        dx[rows, :] = out
        dxb[rows, :] = out.astype(BF16)
        return eights(d * nn), eights(d)

    small[...] = jnp.zeros_like(small)
    return put_smalls(small, 0, rows_sum(dy.shape[0], 64, dy.shape[1], through, 2))


def cross_backward_kernel(
    crop, dt2, dmem_in, normal, inv, gains, out_t, lse, q, pairs, t1b, memory, wq, wm, wo,
    dt1, dmem, grads, small,
    mask, dx, dxb, do, do_t, q_t, keys_t, dpairs, dq_t, p_s, ds_s, mem_t, tick,
):
    fill_mask(mask, crop)
    norm_rows_backward(dt2, normal, inv, gains.at[1:2, :], small, dx, dxb)
    tick(0.8)
    put_panels(grads, 0, out_t[...].astype(BF16), dxb, tick, 0.7)
    do[...] = mm_nt(dxb[...], wo[...]).astype(BF16)
    do_t[...] = do[...].T
    q_t[...] = q[...].T
    keys_t[...] = pairs[:, :512].T
    tick(1.2)
    attend_backward(
        pairs.at[:, 0:512], pairs.at[:, 512:1024], keys_t, q, q_t, do, do_t, out_t, lse, mask, False,
        dpairs.at[:, 0:512], dpairs.at[:, 512:1024], dq_t, p_s, ds_s, tick, 10.0,
    )
    dq = dq_t[...].T
    put_panels(grads, 1024, t1b[...].T, dq, tick, 0.8)
    dt1[...] = dx[...] + mm_nt(dq, wq[...])
    mem_t[...] = memory[...].T
    put_panels(grads, 2048, mem_t, dpairs, tick, 1.8)
    dmem[...] = dmem_in[...] + mm_nt(dpairs[...], wm[...])
    tick(1.5)


def self_backward(dy, normal, inv, gain, out_t, lse, q, keys, v, xb, w, wo, mask, causal, grads, small,
                  dx, dxb, do, do_t, q_t, keys_t, dqkv, dq_t, p_s, ds_s, tick, cost):
    at = norm_rows_backward(dy, normal, inv, gain, small, dx, dxb)
    tick(1.0)
    put_panels(grads, 0, out_t[...].astype(BF16), dxb, tick, 0.8)
    do[...] = mm_nt(dxb[...], wo[...]).astype(BF16)
    do_t[...] = do[...].T
    q_t[...] = q[...].T
    keys_t[...] = keys[...].T
    tick(1.2)
    attend_backward(
        keys, v, keys_t, q, q_t, do, do_t, out_t, lse, mask, causal,
        dqkv.at[:, 512:1024], dqkv.at[:, 1024:1536], dq_t, p_s, ds_s, tick, cost,
    )
    dqkv[:, 0:512] = dq_t[...].T
    put_panels(grads, 1024, xb[...].T, dqkv, tick, 2.4)
    dx[...] += mm_nt(dqkv[...], w[...])
    tick(1.5)
    return at


def tag_backward_kernel(
    dt1, normal, inv, gains, out_t, lse, q, keys, v, t0b, ids, w, wo,
    grads, small,
    mask, dx, dxb, do, do_t, q_t, keys_t, dqkv, dq_t, p_s, ds_s, tick,
):
    at = self_backward(
        dt1, normal, inv, gains.at[0:1, :], out_t, lse, q, keys, v, t0b, w, wo, mask, True, grads, small,
        dx, dxb, do, do_t, q_t, keys_t, dqkv, dq_t, p_s, ds_s, tick, 5.5,
    )
    vocab = (small.shape[0] - at) // 2
    hot = hot_columns(ids[lax.axis_index(SECTION)], 32).astype(BF16)
    put_small(small, at, mm(hot, dx[...].astype(BF16)))


def encoder_feed_backward_kernel(
    dmem, normal, inv, gain, u, gu, h, wu, wd,
    dh, grads, small,
    db, dz, dx, t_s, tick,
):
    up_rows = 512 * wu.shape[1] // PANEL
    small[...] = jnp.zeros_like(small)
    feed_backward(
        dmem, db, normal, inv, gain, u, gu, h, wu, wd,
        grads.at[0:up_rows, :], grads.at[up_rows : 2 * up_rows, :], small, dh, dz, dx, t_s, tick,
    )


def encoder_attention_backward_kernel(
    crop, dh, normal, inv, gain, out_t, lse, q, keys, v, eb, w, wo,
    de, grads, small,
    mask, dhb, dxb, do, do_t, q_t, keys_t, dqkv, dq_t, p_s, ds_s, tick,
):
    fill_mask(mask, crop)
    dhb[...] = dh[...].astype(BF16)
    self_backward(
        dhb, normal, inv, gain, out_t, lse, q, keys, v, eb, w, wo, mask, False, grads, small,
        de, dxb, do, do_t, q_t, keys_t, dqkv, dq_t, p_s, ds_s, tick, 17.0,
    )


def spread_rows(value, pad):
    n = value.shape[0]
    pad[0:PITCH, :] = jnp.zeros((PITCH, pad.shape[1]), BF16)
    pad[PITCH : n + PITCH, :] = value
    pad[n + PITCH :, :] = jnp.zeros((PITCH, pad.shape[1]), BF16)


def conv_weight_grad(value, dz_pad, grads, base, tick):
    n = value.shape[0]
    for dx in range(3):
        shifted = value if dx == 1 else pltpu.roll(value, (1 - dx) % n, 0)
        shifted_t = shifted.astype(BF16).T
        for dy in range(3):
            part = mm(shifted_t, dz_pad[(2 - dy) * PITCH : (2 - dy) * PITCH + n, :])
            at = base + (dy * 3 + dx) * PANEL
            grads[at : at + PANEL, :] = part.astype(BF16)
        tick(1.0)


def conv_input_grad(cols, w, n, tick):
    total = None
    for dy in range(3):
        for dx in range(3):
            tap = dy * 3 + dx
            rows = slice((2 - dy) * PITCH, (2 - dy) * PITCH + n)
            lanes = slice((2 - dx) * PANEL, (3 - dx) * PANEL)
            part = mm_nt(cols[rows, lanes], w[tap * PANEL : (tap + 1) * PANEL, :])
            total = part if total is None else total + part
    return total


def front_backward(
    crop, de, feat, y1, g1, y2, g2, w1, w2, wp, dfeat, grads_a, grads_b, small, done_a, done_b,
    deb, z, x, first_in, wide, cols, pad, tick,
):
    n = x.shape[0]
    s = own_side(crop)
    small[...] = jnp.zeros_like(small)

    def take(rows):
        d = de[rows, :]
        deb[rows, :] = d.astype(BF16)
        return (eights(d),)

    at = put_small(small, 0, rows_sum(n, 64, de.shape[1], take)[0])
    put_panels(grads_a, 0, y2[...].T, deb, tick, 0.6)
    z[...] = mm_nt(deb[...], wp[...])

    def second(rows):
        d = z[rows, :] * g2[rows, :].astype(F32)
        z[rows, :] = d
        return (eights(d),)

    at = put_small(small, at, rows_sum(n, 64, PANEL, second)[0])
    im2col(z[...], cols)
    spread_rows(z[...].astype(BF16), pad)
    x[...] = z[...]
    tick(1.0)
    conv_weight_grad(y1[...].astype(F32), pad, grads_a, 2 * wp.shape[0], tick)
    done_a()
    z[...] = conv_input_grad(cols, w2, n, tick)
    tick(2.5)

    def first(rows):
        d = z[rows, :] * g1[rows, :].astype(F32)
        z[rows, :] = d
        return (eights(d),)

    put_small(small, at, rows_sum(n, 64, PANEL, first)[0])
    spread_rows(z[...].astype(BF16), pad)
    wide[...] = feat[...].astype(F32)
    first_in[...] = jnp.zeros_like(first_in)
    for r in range(GRID):
        first_in[r * PITCH : r * PITCH + GRID, :] = wide[r * GRID : (r + 1) * GRID, :]
    first_in[...] = jnp.where(inside_rows(0, n, PANEL, s), first_in[...], 0.0)
    tick(1.0)
    conv_weight_grad(first_in[...], pad, grads_b, 0, tick)
    done_b()
    im2col(z[...], cols)
    tick(0.5)
    x[...] = jnp.where(inside_rows(0, n, PANEL, s), x[...] + conv_input_grad(cols, w1, n, tick), 0.0)
    tick(2.5)
    for r in range(GRID):
        wide[r * GRID : (r + 1) * GRID, :] = x[r * PITCH : r * PITCH + GRID, :]
    dfeat[...] = wide[...].astype(BF16)


class Mesh2:
    def __init__(self, sections, splits):
        self.sections, self.splits = sections, splits
        self.devices = sections * splits
        split_bits = [(SPLIT, 1 << i) for i in range(splits.bit_length() - 1)]
        section_bits = [(SECTION, 1 << i) for i in range(sections.bit_length() - 1)]
        self.core = split_bits[:1]
        self.rest = section_bits + split_bits[1:]
        self.unit = 16 * self.devices

    def orders(self, turn):
        r = self.rest
        if len(r) < 3:
            return [(self.core + r, 1.0)]
        first, second, rest = r[0], r[1], r[2:]
        later = [second, first] if turn % 2 else [first, second]
        return [
            (self.core + [first, second] + rest, 0.38),
            (self.core + rest[:1] + later + rest[1:], 0.24),
            (self.core + [second, first] + rest, 0.38),
        ]

    def links(self, axis, stride):
        if (axis, stride) in self.core:
            return [(0, 1)]
        if axis == SPLIT and self.splits == 16 and stride > 2:
            return [(1, 1)] if stride == 4 else [(1, 1), (2, 2)]
        return [((axis, stride), 1)]

    def padded(self, rows):
        return -(-rows // self.unit) * self.unit

    def cut(self, rows, turn):
        units = rows // self.unit
        streams, at, goal = [], 0, 0.0
        for order, part in self.orders(turn):
            goal += part
            stop = int(round(goal * units))
            if stop > at:
                streams.append((order, at * self.unit, (stop - at) * self.unit))
            at = stop
        return streams


class Share:
    ICI = 45e3
    CORE = 300e3
    LATENCY = 1.8

    def __init__(self, mesh2, total_rows, own, local_sem, send_sem, recv_sem):
        self.mesh2 = mesh2
        self.own, self.local_sem, self.send_sem, self.recv_sem = own, local_sem, send_sem, recv_sem
        everyone = mesh2.core + mesh2.rest
        self.bits = len(everyone)
        place = {SECTION: lax.axis_index(SECTION), SPLIT: lax.axis_index(SPLIT)}
        self.bit_of, self.partner_of = {}, {}
        for axis, stride in everyone:
            bit = lax.rem(lax.div(place[axis], np.int32(stride)), np.int32(2))
            moved = dict(place)
            moved[axis] = moved[axis] + stride - 2 * stride * bit
            self.bit_of[(axis, stride)] = bit
            self.partner_of[(axis, stride)] = (moved[SECTION], moved[SPLIT])
        self.streams = []
        self.own_rows = 0
        self.turn = -1
        self.clock = 0.0
        self.free = {}
        self.queue = []

    def bit(self, axis, stride):
        return self.bit_of[(axis, stride)]

    def partner(self, axis, stride):
        return self.partner_of[(axis, stride)]

    def enter(self):
        barrier = pltpu.get_barrier_semaphore()
        everyone = self.mesh2.core + self.mesh2.rest
        for axis, stride in everyone:
            pl.semaphore_signal(
                barrier, inc=1, device_id=self.partner(axis, stride), device_id_type=pl.DeviceIdType.MESH
            )
        pl.semaphore_wait(barrier, len(everyone))

    def add(self, source, total, landing, base_of_landing):
        members = []
        self.turn += 1
        for order, base, rows in self.mesh2.cut(total.shape[0], self.turn):
            i = len(self.streams)
            self.streams.append(
                dict(
                    source=source, total=total, landing=landing, base=base, land=base_of_landing + base, rows=rows,
                    order=order, own=self.own_rows, step=0,
                )
            )
            self.own_rows += rows >> self.bits
            members.append(i)
            self.send(i, 0)
        return members

    def kept(self, stream, t):
        if t == 0:
            return stream["source"], stream["base"]
        return stream["landing"], stream["land"] + stream["rows"] - (stream["rows"] >> (t - 1))

    def off(self, stream, t):
        at = stream["base"]
        for level in range(t):
            at = at + self.bit(*stream["order"][level]) * (stream["rows"] >> (level + 1))
        return pl.multiple_of(at, 16)

    def copy(self, i, t):
        stream = self.streams[i]
        if t < self.bits:
            axis, stride = stream["order"][t]
            half = stream["rows"] >> (t + 1)
            src, at = self.kept(stream, t)
            dst, landed = self.kept(stream, t + 1)
            src = src.at[pl.ds(pl.multiple_of(at + (1 - self.bit(axis, stride)) * half, 16), half), :]
            dst = dst.at[pl.ds(landed, half), :]
        else:
            level = 2 * self.bits - 1 - t
            axis, stride = stream["order"][level]
            size = stream["rows"] >> (level + 1)
            src = dst = stream["total"].at[pl.ds(self.off(stream, level + 1), size), :]
            if t == self.bits:
                src = self.own.at[pl.ds(stream["own"], size), :]
        return pltpu.make_async_remote_copy(
            src_ref=src,
            dst_ref=dst,
            send_sem=self.send_sem.at[i],
            recv_sem=self.recv_sem.at[i, t],
            device_id=self.partner(axis, stride),
            device_id_type=pl.DeviceIdType.MESH,
        )

    def keep_own(self, i):
        stream = self.streams[i]
        size = stream["rows"] >> self.bits
        return pltpu.make_async_copy(
            self.own.at[pl.ds(stream["own"], size), :],
            stream["total"].at[pl.ds(self.off(stream, self.bits), size), :],
            self.local_sem.at[i],
        )

    def send(self, i, t):
        stream = self.streams[i]
        self.copy(i, t).start()
        level = t if t < self.bits else 2 * self.bits - 1 - t
        size = (stream["rows"] >> (level + 1)) * PANEL * 2
        links = self.mesh2.links(*stream["order"][level])
        start = max([self.clock] + [self.free.get(link, 0.0) for link, _ in links])
        end = start
        for link, times in links:
            self.free[link] = start + times * size / (self.ICI if link else self.CORE)
            end = max(end, self.free[link])
        self.queue.append((end + self.LATENCY, i, t))

    def event(self, i, t):
        stream = self.streams[i]
        copy = self.copy(i, t)
        copy.wait_recv()
        if t < self.bits:
            axis, stride = stream["order"][t]
            half = stream["rows"] >> (t + 1)
            src, at = self.kept(stream, t)
            own = at + self.bit(axis, stride) * half
            landing, landed = self.kept(stream, t + 1)
            last = t + 1 == self.bits
            dst, to = (self.own, stream["own"]) if last else (landing, landed)
            def add_rows(first, count):
                tile = next(v for v in (128, 64, 32, 16) if count % v == 0)

                def add(k, carry):
                    mine = src[pl.ds(pl.multiple_of(own + first + k * tile, 16), tile), :]
                    other = landing[pl.ds(pl.multiple_of(landed + first + k * tile, 16), tile), :]
                    dst[pl.ds(pl.multiple_of(to + first + k * tile, 16), tile), :] = mine + other
                    return carry

                lax.fori_loop(0, count // tile, add, 0)

            if last:
                add_rows(0, half)
                self.keep_own(i).start()
                copy.wait_send()
                self.send(i, t + 1)
            else:
                quarter = half // 2
                ahead = self.bit(*stream["order"][t + 1]) * quarter
                add_rows(quarter - ahead, quarter)
                copy.wait_send()
                self.send(i, t + 1)
                add_rows(ahead, quarter)
        else:
            if t == self.bits:
                self.keep_own(i).wait()
            copy.wait_send()
            if t + 1 < 2 * self.bits:
                self.send(i, t + 1)
        stream["step"] = t + 1

    def next(self):
        when, i, t = min(self.queue)
        self.queue.remove((when, i, t))
        self.clock = max(self.clock, when)
        self.event(i, t)

    def tick(self, cost):
        goal = self.clock + cost
        while self.queue and min(self.queue)[0] <= goal:
            self.next()
        self.clock = goal

    def until_sent(self, members):
        while any(self.streams[i]["step"] == 0 for i in members):
            self.next()

    def drain(self):
        while self.queue:
            self.next()


def stage(share, crop, ins, scratch, body):
    count = len(ins)

    def inner(*refs):
        loaded, sems, work = refs[:count], refs[count], refs[count + 1 :]
        copies = [pltpu.make_async_copy(a, b, sems.at[i]) for i, (a, b) in enumerate(zip(ins, loaded))]
        for copy in copies:
            copy.start()
        share.tick(1.5)
        for copy in copies:
            copy.wait()
        body(loaded, work)

    pl.run_scoped(
        inner,
        *[pltpu.VMEM(ref.shape, ref.dtype) for ref in ins],
        pltpu.SemaphoreType.DMA((count,)),
        *[pltpu.VMEM(shape, dtype) for shape, dtype in scratch],
    )


def backward_kernel(mesh2, rows, counts, crop, ids, *refs):
    groups, at = [], 0
    for count in counts:
        groups.append(refs[at : at + count])
        at += count
    box_in, cross_in, tag_in, feed_in, att_in, front_in, (boxes, dfeat), totals = groups
    source_0, source_a, source_b, landing, own, small, dt, dm, dh, local_sem, send_sem, recv_sem = refs[at:]
    n, width = dm.shape
    count = dt.shape[0]
    hidden = feed_in[3].shape[1]
    share = Share(mesh2, rows, own, local_sem, send_sem, recv_sem)
    tick = share.tick
    share.enter()
    lands = [sum(rows[:i]) for i in range(len(rows))]

    def begin(i, src):
        return share.add(src, totals[i], landing, lands[i])

    parts, at = [], 0
    for size in (24, 8, 72, 16, 8, 8):
        parts.append(small.at[at : at + size, :])
        at += size
    small[at:, :] = jnp.zeros((small.shape[0] - at, PANEL), F32)
    feeds = [None, None]

    def attend_scratch(queries, keys, times):
        return [((n, PANEL), F32)] + [
            ((queries, width), BF16), ((queries, width), BF16), ((width, queries), BF16), ((width, queries), BF16),
            ((width, keys), BF16), ((keys, times * width), BF16), ((width, queries), BF16),
            ((keys, queries), BF16), ((keys, queries), BF16),
        ]

    def box(loaded, work):
        def box_done():
            begin(0, source_0)

        box_kernel(crop, *loaded, boxes, dt, dm, source_0, source_b, parts[0], *work, box_done=box_done, tick=tick)

    tall, cell_count = (count, width), boxes.shape[1]
    stage(
        share, crop, box_in,
        [(tall, BF16), ((count, hidden), BF16), ((count, hidden), BF16), (tall, BF16), ((count, 1), F32), (tall, F32),
         ((count, hidden), BF16), (tall, F32), ((512, count), BF16), (tall, F32), (tall, BF16),
         ((cell_count, count), BF16), ((count, cell_count), BF16), ((cell_count, width), F32), ((cell_count, width), F32),
         ((1, n), F32), ((cell_count, n), F32), ((n, 2 * width), BF16), ((width, n), BF16)],
        box,
    )
    feeds[1] = begin(1, source_b)

    def cross(loaded, work):
        cross_backward_kernel(
            crop, dt, dm, *loaded, dt, dm, source_a, parts[1], work[0], dt, *work[1:], tick=tick
        )

    stage(share, crop, cross_in, attend_scratch(count, n, 2) + [((width, n), BF16)], cross)
    feeds[0] = begin(2, source_a)
    share.until_sent(feeds[1])

    def tags(loaded, work):
        tag_backward_kernel(
            dt, *loaded[:9], ids, *loaded[9:], source_b, parts[2], work[0], dt, *work[1:], tick=tick
        )

    stage(share, crop, tag_in, attend_scratch(count, count, 3), tags)
    feeds[1] = begin(3, source_b)
    share.until_sent(feeds[0])

    def feed(loaded, work):
        encoder_feed_backward_kernel(dm, *loaded, dh, source_a, parts[3], *work, tick=tick)

    stage(share, crop, feed_in, [((n, width), BF16), ((n, hidden), BF16), ((n, width), F32), ((512, n), BF16)], feed)
    feeds[0] = begin(4, source_a)
    share.until_sent(feeds[1])

    def attention(loaded, work):
        encoder_attention_backward_kernel(
            crop, dh, *loaded, dm, source_b, parts[4], work[0], work[1], *work[2:], tick=tick
        )

    scratch = attend_scratch(n, n, 3)
    stage(share, crop, att_in, scratch[:1] + [((n, width), BF16)] + scratch[1:], attention)
    feeds[1] = begin(5, source_b)
    share.until_sent(feeds[0])

    def front(loaded, work):
        feat, y1 = loaded[0], loaded[1]
        channels = y1.shape[1]

        def done_a():
            feeds[0] = begin(6, source_a)
            share.until_sent(feeds[1])

        def done_b():
            at = 9 * channels
            source_b[at : at + small.shape[0], :] = small[...].astype(BF16)
            begin(7, source_b)

        front_backward(
            crop, dm, *loaded, dfeat, source_a, source_b, parts[5], done_a, done_b, *work, tick=tick
        )

    channels = front_in[1].shape[1]
    stage(
        share, crop, front_in,
        [((n, width), BF16), ((n, channels), F32), ((n, channels), F32), ((n, channels), F32), (front_in[0].shape, F32),
         ((n + 64, 768), BF16), ((n + 64, channels), BF16)],
        front,
    )
    share.drain()


def cost_of(us):
    return pl.CostEstimate(flops=int(us * 1.1e9), bytes_accessed=int(us * 3.6e6), transcendentals=0)


def run(name, body, ins, outs, scratch, smem=0, us=10.0):
    shapes = [jax.ShapeDtypeStruct(shape, dtype) for shape, dtype in outs]
    fetched = ins[smem:]
    counts = [smem, len(fetched), len(outs), len(fetched), len(outs), len(scratch)]

    def whole(*refs):
        groups, at = [], 0
        for count in counts:
            groups.append(refs[at : at + count])
            at += count
        scalars, sources, targets, in_refs, out_refs, work = groups
        in_sem, out_sem = refs[at:]
        def load(i):
            return pltpu.make_async_copy(sources[i], in_refs[i], in_sem.at[i])

        def store(i):
            return pltpu.make_async_copy(out_refs[i], targets[i], out_sem.at[i])

        for i in range(len(in_refs)):
            load(i).start()
        here, gone = set(), set()

        def need(*wanted):
            for i, ref in enumerate(in_refs):
                if i not in here and any(ref is other for other in wanted):
                    load(i).wait()
                    here.add(i)

        def done(*ready):
            for i, ref in enumerate(out_refs):
                if i not in gone and any(ref is other for other in ready):
                    store(i).start()
                    gone.add(i)

        body(*scalars, *in_refs, *out_refs, *work, need=need, done=done)
        need(*in_refs)
        done(*out_refs)
        for i in range(len(out_refs)):
            store(i).wait()

    return pl.pallas_call(
        whole,
        out_shape=shapes,
        in_specs=[pl.BlockSpec(memory_space=pltpu.SMEM if i < smem else pltpu.HBM) for i in range(len(ins))],
        out_specs=[pl.BlockSpec(memory_space=pltpu.HBM)] * len(outs),
        scratch_shapes=[pltpu.VMEM(v.shape, v.dtype) for v in fetched]
        + [pltpu.VMEM(v.shape, v.dtype) for v in shapes]
        + [pltpu.VMEM(shape, dtype) for shape, dtype in scratch]
        + [pltpu.SemaphoreType.DMA((len(fetched),)), pltpu.SemaphoreType.DMA((len(outs),))],
        compiler_params=pltpu.CompilerParams(vmem_limit_bytes=VMEM_LIMIT),
        cost_estimate=cost_of(us),
        name=name,
    )(*ins)


def position_rows(count, width):
    places = np.arange(count, dtype=np.float32)[:, None]
    factor = np.exp(np.arange(width // 2, dtype=np.float32) * np.float32(-2.0 * math.log(10000.0) / width))
    angles = (places * factor.astype(np.float32)[None, :]).astype(np.float32)
    return np.concatenate([np.sin(angles), np.cos(angles)], axis=1).astype(np.float32)


def unpack_kernel(plan, small_plan, pack_count, *refs):
    packs = refs[:pack_count]
    out_count = len(plan) + len(small_plan)
    outs = refs[pack_count : pack_count + out_count]
    buffers = refs[pack_count + out_count : pack_count + out_count + pack_count]
    stages = refs[pack_count + out_count + pack_count : -2]
    in_sem, out_sem = refs[-2:]
    loads = [
        pltpu.make_async_copy(pack, buffer, in_sem.at[i]) for i, (pack, buffer) in enumerate(zip(packs, buffers))
    ]
    for load in loads:
        load.start()
    stores = []
    ready = set()
    for i, (group, base, rows, panels) in enumerate(plan):
        if group not in ready:
            loads[group].wait()
            ready.add(group)
        for c in range(panels):
            stages[i][:, c * PANEL : (c + 1) * PANEL] = buffers[group][base + c * rows : base + (c + 1) * rows, :].astype(F32)
        store = pltpu.make_async_copy(stages[i], outs[i], out_sem.at[i])
        store.start()
        stores.append(store)
    if pack_count - 1 not in ready:
        loads[-1].wait()
    for k, pieces in enumerate(small_plan):
        i = len(plan) + k
        for to, base, rows, width in pieces:
            start = base // 16 * 16
            stop = -(-(base + rows * width // PANEL) // 16) * 16
            block = buffers[-1][start:stop, :].astype(F32)
            for c in range(width // PANEL):
                at = base - start + c * rows
                stages[i][to : to + rows, c * PANEL : (c + 1) * PANEL] = block[at : at + rows, :]
        store = pltpu.make_async_copy(stages[i], outs[i], out_sem.at[i])
        store.start()
        stores.append(store)
    for store in stores:
        store.wait()


def train(mesh2, features, crop_side, tag_ids, tag_count, cell_pick, box_units, weights):
    (
        conv_first, conv_first_bias, conv_second, conv_second_bias, projection, projection_bias,
        encoder_attention, encoder_output, attention_gain, attention_shift,
        encoder_up, encoder_up_bias, encoder_down, encoder_down_bias, feedforward_gain, feedforward_shift,
        tag_table, decoder_attention, decoder_output, decoder_query, decoder_memory, decoder_cross,
        decoder_up, decoder_up_bias, decoder_down, decoder_down_bias, decoder_gain, decoder_shift,
        box_query, box_memory, box_output, box_hidden, box_hidden_bias, box_coord,
    ) = weights
    feature_map = features[0, 0]
    n = GRID * PITCH
    cells_in, channels = feature_map.shape
    width = projection.shape[1]
    hidden = encoder_up.shape[1]
    count = tag_ids.shape[2]
    cell_count = cell_pick.shape[2]
    vocab = tag_table.shape[0]

    def row(v):
        return v.reshape(1, -1)

    def packed(rows):
        return ((mesh2.padded(rows), PANEL), BF16)

    cell_positions = np.zeros((GRID, PITCH, width), np.float32)
    cell_positions[:, :GRID] = position_rows(GRID * GRID, width).reshape(GRID, GRID, width)
    cell_positions = jnp.asarray(cell_positions.reshape(n, width))
    tag_positions = jnp.asarray(position_rows(count, width))

    big, tall = (n, width), (count, width)
    stats = [((width, n), F32), ((HEADS, 1, n), F32), (big, BF16), ((n, 1), F32)]
    tag_stats = [((width, count), F32), ((HEADS, 1, count), F32), (tall, BF16), ((count, 1), F32)]
    ins = [
        [feature_map, conv_first, row(conv_first_bias), conv_second, row(conv_second_bias), projection, row(projection_bias),
         cell_positions],
        [encoder_attention, encoder_output, row(attention_gain), row(attention_shift)],
        [encoder_up, row(encoder_up_bias), encoder_down, row(encoder_down_bias), row(feedforward_gain),
         row(feedforward_shift), decoder_memory, box_memory],
        [tag_ids, tag_table, tag_positions, decoder_attention, decoder_output, decoder_gain, decoder_shift],
        [decoder_query, decoder_cross],
    ]
    outs = [
        [((n, channels), BF16)] * 4,
        [(big, BF16)] * 4 + stats + [(big, BF16)],
        [((n, hidden), BF16)] * 2 + [(big, BF16), ((n, 1), F32), (big, BF16)] + [((n, 2 * width), BF16)] * 2,
        [(tall, BF16)] * 4 + tag_stats,
        [(tall, BF16)] * 2 + tag_stats + [(tall, F32)],
    ]
    (
        y1, g1, y2, g2,
        eb, eq, ek, ev, eo, else_, en, ei, h,
        u, gu, fn, fi, memory, pairs, box_pairs,
        t0b, tq, tk, tv, to, tlse, tn, ti,
        t1b, cq, co, clse, cn, ci, t2,
    ) = run(
        "forward", functools.partial(forward_kernel, [len(g) for g in ins] + [len(g) for g in outs]),
        [crop_side] + [v for g in ins for v in g], [v for g in outs for v in g], [(big, F32), (tall, F32)], 1, us=80.0,
    )
    up_rows = width * hidden // PANEL
    sq_rows = width * width // PANEL
    coord16 = jnp.pad(box_coord.T, ((0, 12), (0, 0)))
    conv_rows = 9 * channels
    groups = [
        [tag_count, t2, decoder_up, row(decoder_up_bias), decoder_down, row(decoder_down_bias), decoder_gain,
         decoder_shift, cell_pick, box_units, box_pairs, memory,
         box_query, box_memory, box_output, box_hidden, row(box_hidden_bias), coord16],
        [cn, ci, decoder_gain, co, clse, cq, pairs, t1b, memory, decoder_query, decoder_memory, decoder_cross],
        [tn, ti, decoder_gain, to, tlse, tq, tk, tv, t0b, decoder_attention, decoder_output],
        [fn, fi, row(feedforward_gain), u, gu, h, encoder_up, encoder_down],
        [en, ei, row(attention_gain), eo, else_, eq, ek, ev, eb, encoder_attention, encoder_output],
        [feature_map, y1, g1, y2, g2, conv_first, conv_second, projection],
    ]
    small_rows = 144
    rows = [5 * sq_rows, 2 * up_rows, 4 * sq_rows, 4 * sq_rows, 2 * up_rows, 4 * sq_rows, 2 * channels + conv_rows, conv_rows + small_rows]
    rows = [mesh2.padded(r) for r in rows]
    streams = sum(len(mesh2.cut(r, turn)) for turn, r in enumerate(rows))
    bits = len(mesh2.core + mesh2.rest)
    flat = [v for group in groups for v in group]
    spaces = [pltpu.SMEM, pltpu.VMEM] + [pl.ANY] * len(flat)
    boxes, dfeat, *packs = pl.pallas_call(
        functools.partial(backward_kernel, mesh2, rows, [len(g) for g in groups] + [2, len(rows)]),
        out_shape=[jax.ShapeDtypeStruct((4, cell_count), F32), jax.ShapeDtypeStruct((cells_in, channels), BF16)] + [jax.ShapeDtypeStruct((r, PANEL), BF16) for r in rows],
        in_specs=[pl.BlockSpec(memory_space=space) for space in spaces],
        out_specs=[pl.BlockSpec(memory_space=pltpu.VMEM)] * 2 + [pl.BlockSpec(memory_space=pl.ANY)] * len(rows),
        scratch_shapes=[
            pltpu.VMEM((rows[0], PANEL), BF16),
            pltpu.VMEM((max(rows[1:]), PANEL), BF16),
            pltpu.VMEM((max(rows[1:]), PANEL), BF16),
            pltpu.VMEM((sum(rows), PANEL), BF16),
            pltpu.VMEM((sum(rows) // mesh2.devices, PANEL), BF16),
            pltpu.VMEM((small_rows, PANEL), F32),
            pltpu.VMEM(tall, F32), pltpu.VMEM(big, F32), pltpu.VMEM(big, F32),
            pltpu.SemaphoreType.DMA((streams,)),
            pltpu.SemaphoreType.DMA((streams,)),
            pltpu.SemaphoreType.DMA((streams, 2 * bits)),
        ],
        compiler_params=pltpu.CompilerParams(vmem_limit_bytes=VMEM_LIMIT, collective_id=1, has_side_effects=True),
        cost_estimate=cost_of(180.0),
        name="backward",
    )(crop_side, tag_ids, *flat)
    plan = {
        31: (0, 0, width, 2), 30: (0, sq_rows, width, 2), 28: (0, 2 * sq_rows, width, 2), 29: (0, 3 * sq_rows, width, 4),
        22: (1, 0, width, hidden // PANEL), 24: (1, up_rows, hidden, 2),
        21: (2, 0, width, 2), 19: (2, sq_rows, width, 2), 20: (2, 2 * sq_rows, width, 4),
        18: (3, 0, width, 2), 17: (3, sq_rows, width, 6),
        10: (4, 0, width, hidden // PANEL), 12: (4, up_rows, hidden, 2),
        7: (5, 0, width, 2), 6: (5, sq_rows, width, 6),
        4: (6, 0, channels, 2), 2: (6, 2 * channels, conv_rows, 1), 0: (7, 0, conv_rows, 1),
    }
    one, up = width // PANEL, hidden // PANEL
    at_box = conv_rows
    at_cross = at_box + 24
    at_tag = at_cross + 8
    at_feed = at_tag + 72
    at_att = at_feed + 16
    at_front = at_att + 8
    small_plan = {
        26: [(2, at_box, 1, width), (1, at_cross, 1, width), (0, at_tag, 1, width)],
        27: [(2, at_box + one, 1, width), (1, at_cross + one, 1, width), (0, at_tag + one, 1, width)],
        25: [(0, at_box + 2 * one, 1, width)], 23: [(0, at_box + 3 * one, 1, hidden)],
        32: [(0, at_box + 3 * one + up, 1, width)], 33: [(0, at_box + 4 * one + up, 4, width)],
        16: [(0, at_tag + 2 * one, vocab, width)],
        14: [(0, at_feed, 1, width)], 15: [(0, at_feed + one, 1, width)],
        13: [(0, at_feed + 2 * one, 1, width)], 11: [(0, at_feed + 3 * one, 1, hidden)],
        8: [(0, at_att, 1, width)], 9: [(0, at_att + one, 1, width)],
        5: [(0, at_front, 1, width)], 3: [(0, at_front + one, 1, channels)], 1: [(0, at_front + one + 1, 1, channels)],
    }
    shapes = [weights[k].shape for k in plan]
    shapes += [(sum(rows for _, _, rows, _ in pieces), pieces[0][3]) for pieces in small_plan.values()]
    outs = pl.pallas_call(
        functools.partial(unpack_kernel, list(plan.values()), list(small_plan.values()), len(packs)),
        out_shape=[jax.ShapeDtypeStruct(shape, F32) for shape in shapes],
        in_specs=[pl.BlockSpec(memory_space=pl.ANY)] * len(packs),
        out_specs=[pl.BlockSpec(memory_space=pl.ANY)] * len(shapes),
        scratch_shapes=[pltpu.VMEM(p.shape, BF16) for p in packs]
        + [pltpu.VMEM(shape, F32) for shape in shapes]
        + [pltpu.SemaphoreType.DMA((len(packs),)), pltpu.SemaphoreType.DMA((len(shapes),))],
        compiler_params=pltpu.CompilerParams(vmem_limit_bytes=VMEM_LIMIT),
        name="unpack",
    )(*packs)
    found = dict(zip(list(plan) + list(small_plan), outs))
    found[33] = found[33].T
    result = [found[k].reshape(weight.shape) for k, weight in enumerate(weights)]
    return tuple([boxes[None, None], dfeat[None, None]] + result)


def solution(mesh):
    mesh2 = Mesh2(mesh.shape[SECTION], mesh.shape[SPLIT])

    def local(features, crop_side, tag_ids, tag_count, cell_pick, box_units, *weights):
        return train(mesh2, features, crop_side, tag_ids, tag_count, cell_pick, box_units, weights)

    in_specs = (
        P(SECTION, SPLIT, None, None), P(), P(None, SPLIT, None), P(None, SPLIT), P(None, SPLIT, None),
        P(None, SPLIT, None, None),
    ) + (P(),) * 34
    out_specs = (P(SECTION, SPLIT, None, None),) * 2 + (P(),) * 34
    return jax.shard_map(local, mesh=mesh, in_specs=in_specs, out_specs=out_specs, check_vma=False)
```
